32 devices in a mesh: groups: 2 (over y), replica: 8 (over z, x), tensor: 2 (over core).
Axes of the slice: x: 2, y: 2, z: 4, core: 2. Of those that a mesh axis runs over, the one named last changes fastest.
Arguments:
- hidden: bfloat16 [4, 1024, 4096], P(None, ('groups', 'replica'), 'tensor'), parts along dimension 1, may hold values from -6 to 6
- query_key_value_weight: bfloat16 [4096, 384], P('tensor'), may hold values from -0.09375 to 0.09375
- adapter_down_weight: bfloat16 [16, 4096, 32], P('replica', 'tensor'), may hold values from -0.09375 to 0.09375
- adapter_up_weight: bfloat16 [16, 16, 256], P('replica'), may hold values from -1.5 to 1.5
- key_value_pool: bfloat16 [16, 192, 16, 256], P(('groups', 'replica'), None, 'tensor'), parts along dimension 0, may hold values from -255 to 255
- adapter_replica: int32 [1024, 1], P(('groups', 'replica')), parts along dimension 0, may hold values from 0 to 7; in each aligned block of 64 rows (0 to 63, 64 to 127, ...) at most 16 rows name the same one
- adapter_choice_index: int32 [1024], P(('groups', 'replica')), parts along dimension 0, may hold values from 0 to 1
- cached_length: int32 [16, 64], P(('groups', 'replica')), parts along dimension 0, may hold values from 1 to 48, 1536 in all within a row
- request_block_table: int32 [16, 192], P(('groups', 'replica')), parts along dimension 0, may hold values from 0 to 191, each once within a row
Outputs:
- attn_out: bfloat16 [4, 1024, 128], P(None, ('groups', 'replica')), parts along dimension 1
The draws below stay inside these ranges and needn't reach their ends.
There are 2 independent parts, one for each index of `groups`. The reference program is written for one: setup_inputs(seed, part) draws one part's arguments, and reference() takes and returns one part's arrays. A program takes and returns all parts, laid end to end along the dimension named above; an argument that names none is the same for every part. Nothing has to cross between parts.
Inputs may be any that keep to these rules, and one draw needn't show every extreme that they name: `adapter_replica`: in the rows of one replica no replica is named more than 16 times, a bound that some block reaches. `cached_length`: each row sums to 1536; request j of a replica owns entries j * 3 to j * 3 + 2 of its row of request_block_table. `request_block_table`: each row is a permutation of the replica's 192 blocks.
All inputs are finite; a program needn't handle non-finite values.
Results may differ from the reference program's by a relative error of at most 0.007.
Values may be sent and summed in bfloat16 or wider, within the bound.
A program may use at most 64 MiB of HBM per device.

```python
import math
import jax
import jax.numpy as jnp
import numpy as np
from jax import lax

MODEL_WIDTH = 4096
HEAD_WIDTH = 128
ADAPTER_RANK = 16
STEPS = 4
BLK = 16
MAXB = 3
ADP_DEV = 2
REQ_DEV = 64
CAP = 16
REQS = 512
ADAPTER_COUNT = 16
POOL = 192
TOTAL_LEN = 1536
N_REPLICA = 8


def draw_key_value_pool(key, part):
    key = jax.random.fold_in(key, 11)
    keys = jax.random.split(key, 6)
    array_shape = (N_REPLICA, POOL, BLK, 2 * HEAD_WIDTH)
    base = jnp.clip(jax.random.normal(keys[0], array_shape, jnp.float32), -6.0, 6.0)
    noise = jnp.clip(jax.random.normal(keys[1], (N_REPLICA, POOL, BLK, HEAD_WIDTH), jnp.float32), -2.5, 2.5)
    strength = jnp.exp(jax.random.uniform(keys[2], (N_REPLICA, POOL, 1, 1), jnp.float32, math.log(30.0), math.log(80.0)))
    direction = jnp.clip(jax.random.normal(keys[3], (N_REPLICA, POOL, 1, HEAD_WIDTH), jnp.float32), -2.5, 2.5)
    hot_block = jax.random.uniform(keys[4], (N_REPLICA, POOL, 1, 1), jnp.float32) < 1.0 / 6.0
    hot_slot = jax.random.uniform(keys[5], (N_REPLICA, POOL, BLK, 1), jnp.float32) < 0.3
    strong_key = strength * direction + 0.8 * noise
    key_part = jnp.where(hot_block & hot_slot, strong_key, base[..., :HEAD_WIDTH])
    return jnp.concatenate([key_part, base[..., HEAD_WIDTH:]], axis=-1).astype(jnp.bfloat16)


def plant(array, stream_key, least, top_value):
    index_at = [jax.random.randint(jax.random.fold_in(stream_key, axis), (), 0, length) for axis, length in enumerate(array.shape)]
    main_axis = array.shape.index(max(array.shape))
    neighbour = index_at[:main_axis] + [(index_at[main_axis] + 1) % array.shape[main_axis]] + index_at[main_axis + 1:]
    return array.at[tuple(index_at)].set(least).at[tuple(neighbour)].set(top_value)


def block_levels(own_key, extent, cuts, least, largest):
    level = 1.0
    for dim, parts in cuts:
        heights = jax.random.uniform(jax.random.fold_in(jax.random.fold_in(own_key, 6), dim), (parts,), jnp.float32, least / len(cuts), largest / len(cuts))
        level = level * jnp.repeat(jnp.exp(heights), extent[dim] // parts).reshape((-1,) + (1,) * (len(extent) - 1 - dim))
    return level


def profile(number_of, total, reach, slope):
    loads = [(1 << 20) // math.isqrt(rank ** slope) + 1 for rank in range(2, number_of + 1)]
    spare, counts = total - reach - (number_of - 1), [1] * (number_of - 1)
    while spare > 0:
        candidates = [i for i in range(number_of - 1) if counts[i] < reach]
        whole, left = sum([loads[i] for i in candidates]), spare
        for i in candidates:
            extra = min(reach - counts[i], max(1, left * loads[i] // whole), spare)
            counts[i] = counts[i] + extra
            spare = spare - extra
    return np.array([reach] + counts)


def ragged(key, number_of, total, reach, skew):
    if number_of == 2:
        one = jax.random.randint(key, (), max(1, total - reach), min(reach, total - 1) + 1)
        return jnp.stack([one, total - one])
    sizes = jnp.asarray(profile(number_of, total, reach, skew), jnp.int32)
    twos = (number_of - 1) // 2
    donor, receiver = sizes[1:1 + 2 * twos:2], sizes[2:2 + 2 * twos:2]
    slack = jnp.minimum(donor - 1, reach - receiver)
    moved = jax.random.randint(jax.random.fold_in(key, 1), (twos,), 0, 1 << 20) % (slack + 1)
    sizes = sizes.at[1:1 + 2 * twos:2].set(donor - moved).at[2:2 + 2 * twos:2].set(receiver + moved)
    return sizes[jax.random.permutation(jax.random.fold_in(key, 2), number_of)]


def assign_block(rng, own, number, rows, number_of, top, bound, lean):
    ranking = jax.random.permutation(rng, number_of)
    heavy_load, ordinary = load_shares(number_of, rows * top, bound, lean, True), load_shares(number_of, rows * top, bound, lean, False)
    places = jnp.arange(number_of)

    def named(sizes, offset_by):
        used = int((sizes > 0).sum())
        fixed = max(1, used // 4)
        passed = fixed + (places - fixed + offset_by * (used - fixed)) % max(1, number_of - fixed)
        return jnp.zeros((number_of,), jnp.int32).at[ranking[jnp.where(places < fixed, places, passed)]].set(jnp.asarray(sizes, jnp.int32))

    sizes = jnp.where(number % 4 == 0, named(heavy_load, number // 4), named(ordinary, number - number // 4 - 1))
    mixed = jax.random.permutation(jax.random.fold_in(own, 3), number_of)
    source_of, receiver = mixed[0:number_of // 2 * 2:2], mixed[1:number_of // 2 * 2:2]
    margin = jnp.minimum(sizes[source_of] - 1, bound - sizes[receiver]) // 2
    margin = jnp.where((source_of == ranking[0]) | (receiver == ranking[0]) | (sizes[receiver] == 0), 0, jnp.maximum(margin, 0))
    passed = jax.random.randint(jax.random.fold_in(own, 4), (number_of // 2,), 0, 1 << 20) % (margin + 1)
    sizes = sizes.at[source_of].add(-passed).at[receiver].add(passed)
    labels = jnp.searchsorted(jnp.cumsum(sizes), jnp.arange(rows * top), side="right").astype(jnp.int32)
    grid = labels.reshape(top, rows).T
    grid = grid[jax.random.permutation(jax.random.fold_in(own, 1), rows)]
    offset_by = jax.random.randint(jax.random.fold_in(own, 2), (rows, 1), 0, top)
    return jnp.take_along_axis(grid, (jnp.arange(top)[None, :] + offset_by) % top, axis=1)


def load_shares(number_of, total, most, lean, full):
    weights = [(1 << 20) // math.isqrt(rank ** lean) + 1 for rank in range(1, number_of + 1)]
    largest = most if full else min(most, max(-(-total // number_of), total * weights[0] // sum(weights)))
    least = 1 if total - largest >= number_of - 1 else 0
    given, spare = [largest] + [least] * (number_of - 1), total - largest - least * (number_of - 1)
    while spare > 0:
        candidates = [i for i in range(1, number_of) if given[i] < largest] or [i for i in range(1, number_of) if given[i] < most]
        pool, budget = sum([weights[i] for i in candidates]), spare
        for i in candidates:
            addition = min(most - given[i], max(1, budget * weights[i] // pool), spare)
            given[i] = given[i] + addition
            spare = spare - addition
    return np.array(given)


def normal_values(rng, dims, width, most, shards=(), kind=jnp.bfloat16):
    entries = width * jax.random.normal(rng, dims, jnp.float32)
    if shards:
        entries = entries * block_levels(rng, dims, shards, -0.22, 0.18)
    return jnp.clip(entries, -most, most).astype(kind)


def setup_inputs(seed: int = 0, part: int = 0) -> dict:
    key_of = jax.random.split(jax.random.key(seed), 10)
    own_keys = jax.random.split(jax.random.fold_in(key_of[9], part), 10)
    hidden = normal_values(own_keys[0], (STEPS, REQS, MODEL_WIDTH), 1.0, 6.0, ((1, 8), (2, 2)))
    query_key_value_weight = normal_values(key_of[1], (MODEL_WIDTH, 3 * HEAD_WIDTH), MODEL_WIDTH ** -0.5, 0.09375, ((0, 2),))
    adapter_down_weight = normal_values(key_of[2], (ADAPTER_COUNT, MODEL_WIDTH, 2 * ADAPTER_RANK), MODEL_WIDTH ** -0.5, 0.09375, ((0, 8), (1, 2)))
    adapter_up_weight = normal_values(key_of[3], (ADAPTER_COUNT, ADAPTER_RANK, 2 * HEAD_WIDTH), ADAPTER_RANK ** -0.5, 1.5, ((0, 8),))
    key_value_pool = draw_key_value_pool(jax.random.fold_in(jax.random.fold_in(key_of[9], part), 71), part)
    adapter_replica_keys = jax.random.split(jax.random.fold_in(own_keys[5], 1), REQS // REQ_DEV)
    adapter_replica_turns = jax.random.permutation(jax.random.fold_in(own_keys[5], 3), REQS // REQ_DEV)
    adapter_replica = jax.vmap(lambda own, number: assign_block(jax.random.fold_in(own_keys[5], 2), own, number, REQ_DEV, N_REPLICA, 1, CAP, 2))(adapter_replica_keys, adapter_replica_turns).reshape((REQS, 1))
    adapter_choice_index = plant(jax.random.randint(own_keys[6], (REQS,), 0, ADP_DEV), jax.random.fold_in(own_keys[6], 1), 0, ADP_DEV - 1).astype(jnp.int32)
    cached_length = jax.vmap(lambda own: ragged(own, REQ_DEV, TOTAL_LEN, MAXB * BLK, 2))(jax.random.split(own_keys[7], N_REPLICA)).reshape((N_REPLICA, REQ_DEV)).astype(jnp.int32)
    request_block_table = jax.vmap(lambda own: jax.random.permutation(own, POOL))(jax.random.split(own_keys[8], N_REPLICA)).reshape((N_REPLICA, POOL)).astype(jnp.int32)
    return {"hidden": hidden, "query_key_value_weight": query_key_value_weight, "adapter_down_weight": adapter_down_weight, "adapter_up_weight": adapter_up_weight, "key_value_pool": key_value_pool, "adapter_replica": adapter_replica, "adapter_choice_index": adapter_choice_index, "cached_length": cached_length, "request_block_table": request_block_table}


rope_base = 500000.0
neg_fill = -1e+30

def rotate(vector, position):
    half_len = vector.shape[-1] // 2
    frequency = rope_base ** (-(jnp.arange(half_len, dtype=jnp.float32) * 2.0) / vector.shape[-1])
    angles = position[..., None].astype(jnp.float32) * frequency
    cosine = jnp.cos(angles)
    sine_part = jnp.sin(angles)
    first_part = vector[..., :half_len]
    second = vector[..., half_len:]
    return jnp.concatenate([first_part * cosine - second * sine_part, second * cosine + first_part * sine_part], axis=-1)

def reference(hidden, query_key_value_weight, adapter_down_weight, adapter_up_weight, key_value_pool, adapter_replica, adapter_choice_index, cached_length, request_block_table):
    step_count, total_req, feat_width = hidden.shape
    head_width = HEAD_WIDTH
    per_rep = REQ_DEV
    highest_precision = lax.Precision.HIGHEST
    adapter_slot = (adapter_replica[:, 0] * ADP_DEV + adapter_choice_index).astype(jnp.int32)
    hidden_blocks = jnp.swapaxes(hidden.reshape(step_count, N_REPLICA, per_rep, feat_width), 0, 1)
    adapter_blocks = adapter_slot.reshape(N_REPLICA, per_rep)

    def one_replica(pieces):
        row_payload, selected_rows, seq_lens, table_row, pool_part = pieces
        projected = jnp.dot(row_payload.reshape(step_count * per_rep, feat_width), query_key_value_weight, preferred_element_type=jnp.float32).reshape(step_count, per_rep, 3 * head_width)
        selected_down = adapter_down_weight[selected_rows].astype(jnp.float32)
        reduced_rank = jnp.einsum('snd,ndr->snr', row_payload.astype(jnp.float32), selected_down, precision=highest_precision)
        selected_up = adapter_up_weight[selected_rows].astype(jnp.float32)
        query_term = jnp.einsum('jzv,zvi->jzi', reduced_rank[..., :ADAPTER_RANK], selected_up[..., :head_width], precision=highest_precision)
        value_term = jnp.einsum('jzv,zvi->jzi', reduced_rank[..., ADAPTER_RANK:], selected_up[..., head_width:], precision=highest_precision)
        queries = projected[..., :head_width] + query_term
        key_full = projected[..., head_width:2 * head_width]
        value_full = projected[..., 2 * head_width:] + value_term
        step_ids = jnp.arange(step_count, dtype=jnp.int32)
        position = seq_lens[None, :] + step_ids[:, None]
        query_b = rotate(queries, position).astype(jnp.bfloat16)
        key_b = rotate(key_full, position).astype(jnp.bfloat16)
        value_b = value_full.astype(jnp.bfloat16)
        block_ids = table_row.reshape(per_rep, MAXB)
        cached = pool_part[block_ids].reshape(per_rep, MAXB * BLK, 2 * head_width)
        cache_pos = jnp.arange(MAXB * BLK, dtype=jnp.int32)
        scaling = 1.0 / math.sqrt(head_width)
        old_scores = jnp.einsum('snh,nph->snp', query_b.astype(jnp.float32), cached[..., :head_width].astype(jnp.float32), precision=highest_precision) * scaling
        new_scores = jnp.einsum('snh,tnh->snt', query_b.astype(jnp.float32), key_b.astype(jnp.float32), precision=highest_precision) * scaling
        old_mask = jnp.broadcast_to(cache_pos[None, None, :] < seq_lens[None, :, None], old_scores.shape)
        new_mask = jnp.broadcast_to(step_ids[:, None, None] >= step_ids[None, None, :], new_scores.shape)
        scores = jnp.concatenate([jnp.where(old_mask, old_scores, neg_fill), jnp.where(new_mask, new_scores, neg_fill)], axis=-1)
        all_mask = jnp.concatenate([old_mask, new_mask], axis=-1)
        peak_val = lax.optimization_barrier(jnp.max(scores, axis=-1, keepdims=True))
        weights = jnp.where(all_mask, jnp.exp(scores - peak_val), 0.0)
        total_sum = lax.optimization_barrier(jnp.sum(weights, axis=-1))
        rounded = weights.astype(jnp.bfloat16).astype(jnp.float32)
        length_all = MAXB * BLK
        accum = jnp.einsum('snp,nph->snh', rounded[..., :length_all], cached[..., head_width:].astype(jnp.float32), precision=highest_precision)
        accum = accum + jnp.einsum('snt,tnh->snh', rounded[..., length_all:], value_b.astype(jnp.float32), precision=highest_precision)
        return (accum / total_sum[..., None]).astype(jnp.bfloat16)
    outputs = lax.map(one_replica, (hidden_blocks, adapter_blocks, cached_length, request_block_table, key_value_pool))
    return jnp.swapaxes(outputs, 0, 1).reshape(step_count, total_req, head_width)
```

```python
import functools
import math

import jax
import jax.numpy as jnp
from jax import lax
from jax.experimental import pallas as pl
from jax.experimental.pallas import tpu as pltpu
from jax.sharding import PartitionSpec as P

rope_base = 500000.0
neg_fill = -1e30


def combined_all(part, axis, combine):
    gathered = jax.tree.map(lambda a: lax.all_gather(a, axis), part)

    def take(source):
        return jax.tree.map(lambda a: lax.dynamic_index_in_dim(a, source, 0, False), gathered)

    return lax.fori_loop(
        1, lax.axis_size(axis), lambda source, state: combine(state, take(source)), take(0)
    )


def rotate(vector, position):
    half_len = vector.shape[-1] // 2
    frequency = rope_base ** (-(jnp.arange(half_len, dtype=jnp.float32) * 2.0) / vector.shape[-1])
    angles = position[..., None].astype(jnp.float32) * frequency
    cosine = jnp.cos(angles)
    sine_part = jnp.sin(angles)
    first_part = vector[..., :half_len]
    second = vector[..., half_len:]
    return jnp.concatenate(
        [first_part * cosine - second * sine_part, second * cosine + first_part * sine_part],
        axis=-1,
    )


def adapter_delta(row_payload, choice_index, adapter_down_weight, adapter_up_weight):
    req_count, step_count, feat_width = row_payload.shape
    adapter_rank_width = adapter_up_weight.shape[1]
    head_width = adapter_up_weight.shape[2] // 2
    flattened_rows = row_payload.reshape(req_count * step_count, feat_width)
    summed = jnp.zeros((req_count, step_count, 2 * head_width), jnp.float32)
    highest_precision = lax.Precision.HIGHEST
    for adapter_slot in range(adapter_down_weight.shape[0]):
        reduced_rank = jnp.dot(
            flattened_rows, adapter_down_weight[adapter_slot], preferred_element_type=jnp.float32
        ).reshape(req_count, step_count, 2 * adapter_rank_width)
        up_matrix = adapter_up_weight[adapter_slot].astype(jnp.float32)
        query_term = jnp.einsum(
            "nsr,re->nse",
            reduced_rank[..., :adapter_rank_width],
            up_matrix[:, :head_width],
            precision=highest_precision,
        )
        value_term = jnp.einsum(
            "nsr,re->nse",
            reduced_rank[..., adapter_rank_width:],
            up_matrix[:, head_width:],
            precision=highest_precision,
        )
        chosen = (choice_index == adapter_slot)[:, None, None]
        summed = summed + jnp.where(chosen, jnp.concatenate([query_term, value_term], axis=-1), 0.0)
    return summed


def project_input(row_payload, query_key_value_weight, adapter_term):
    req_count, step_count, feat_width = row_payload.shape
    base_part = jnp.dot(
        row_payload.reshape(req_count * step_count, feat_width),
        query_key_value_weight,
        preferred_element_type=jnp.float32,
    ).reshape(req_count, step_count, -1)
    head_width = adapter_term.shape[-1] // 2
    middle_zeros = jnp.zeros(adapter_term.shape[:-1] + (head_width,), jnp.float32)
    return base_part + jnp.concatenate(
        [adapter_term[..., :head_width], middle_zeros, adapter_term[..., head_width:]], axis=-1
    )


def attend(summed, seq_lens, cached, cache_pos, keep_new):
    head_width = cached.shape[-1] // 2
    step_count = summed.shape[1]
    step_ids = jnp.arange(step_count, dtype=jnp.int32)
    position = seq_lens[:, None] + step_ids[None, :]
    queries = rotate(summed[..., :head_width], position).astype(jnp.bfloat16)
    fresh_k = rotate(summed[..., head_width : 2 * head_width], position).astype(jnp.bfloat16)
    fresh_v = summed[..., 2 * head_width :].astype(jnp.bfloat16)
    scaling = 1.0 / math.sqrt(head_width)
    old_scores = (
        jnp.einsum(
            "nsh,nph->nsp", queries, cached[..., :head_width], preferred_element_type=jnp.float32
        )
        * scaling
    )
    new_scores = (
        jnp.einsum("nsh,nth->nst", queries, fresh_k, preferred_element_type=jnp.float32) * scaling
    )
    old_mask = jnp.broadcast_to(
        cache_pos[None, None, :] < seq_lens[:, None, None], old_scores.shape
    )
    new_mask = jnp.broadcast_to(
        (step_ids[None, :, None] >= step_ids[None, None, :]) & keep_new, new_scores.shape
    )
    old_scores = jnp.where(old_mask, old_scores, neg_fill)
    new_scores = jnp.where(new_mask, new_scores, neg_fill)
    peak_val = jnp.maximum(jnp.max(old_scores, axis=-1), jnp.max(new_scores, axis=-1))
    old_exp = jnp.where(old_mask, jnp.exp(old_scores - peak_val[..., None]), 0.0)
    new_exp = jnp.where(new_mask, jnp.exp(new_scores - peak_val[..., None]), 0.0)
    total_sum = jnp.sum(old_exp, axis=-1) + jnp.sum(new_exp, axis=-1)
    accum = jnp.einsum(
        "nsp,nph->nsh",
        old_exp.astype(jnp.bfloat16),
        cached[..., head_width:],
        preferred_element_type=jnp.float32,
    )
    accum = accum + jnp.einsum(
        "nst,nth->nsh", new_exp.astype(jnp.bfloat16), fresh_v, preferred_element_type=jnp.float32
    )
    return (peak_val, total_sum, accum)


def combine(first_part, second):
    peak_val = jnp.maximum(first_part[0], second[0])
    left_scale = jnp.exp(first_part[0] - peak_val)
    right_scale = jnp.exp(second[0] - peak_val)
    return (
        peak_val,
        first_part[1] * left_scale + second[1] * right_scale,
        first_part[2] * left_scale[..., None] + second[2] * right_scale[..., None],
    )


def serve_rows(value_partial, seq_lens, cached, cache_pos, keep_new):
    summed = lax.psum(value_partial, "tensor")
    stats = attend(summed, seq_lens, cached, cache_pos, keep_new)
    peak_val, total_sum, accum = combined_all(stats, "tensor", combine)
    return (accum / total_sum[..., None]).astype(jnp.bfloat16)


def rows_to_adapters(
    hidden,
    query_key_value_weight,
    adapter_down_weight,
    adapter_up_weight,
    key_value_pool,
    adapter_replica,
    adapter_choice_index,
    cached_length,
    request_block_table,
):
    step_count, req_count, feat_width = hidden.shape
    half_len = key_value_pool.shape[2]
    head_width = key_value_pool.shape[3] // 2
    blocks = request_block_table.shape[1] // req_count
    replica_count = lax.axis_size("replica")
    slot_cap = max(2, (2 * req_count + replica_count - 1) // replica_count)
    tensor_id = lax.axis_index("tensor")
    keep_new = tensor_id == 0
    cache_pos = (
        jnp.arange(blocks, dtype=jnp.int32)[:, None] * (half_len * lax.axis_size("tensor"))
        + tensor_id * half_len
        + jnp.arange(half_len, dtype=jnp.int32)[None, :]
    ).reshape(-1)
    seq_lens = cached_length[0]
    home_rep = adapter_replica[:, 0]
    order_idx = jnp.arange(req_count, dtype=jnp.int32)
    earlier = (home_rep[:, None] == home_rep[None, :]) & (order_idx[None, :] < order_idx[:, None])
    slot_of = home_rep * slot_cap + jnp.sum(earlier.astype(jnp.int32), axis=1)
    slot_total = replica_count * slot_cap
    local_rows = jnp.swapaxes(hidden, 0, 1)
    row_buffer = (
        jnp.zeros((slot_total, step_count, feat_width), hidden.dtype).at[slot_of].set(local_rows)
    )
    cached = key_value_pool[0][request_block_table[0].reshape(req_count, blocks)].reshape(
        req_count, blocks * half_len, 2 * head_width
    )
    cache_buffer = (
        jnp.zeros((slot_total, blocks * half_len, 2 * head_width), key_value_pool.dtype)
        .at[slot_of]
        .set(cached)
    )
    meta_ints = (
        jnp.zeros((slot_total, 2), jnp.int32)
        .at[slot_of]
        .set(jnp.stack([adapter_choice_index, seq_lens], axis=1))
    )
    landed_rows, arrived_cache, landed_integers = (
        lax.all_to_all(row_buffer, "replica", split_axis=0, concat_axis=0, tiled=True),
        lax.all_to_all(cache_buffer, "replica", split_axis=0, concat_axis=0, tiled=True),
        lax.all_to_all(meta_ints, "replica", split_axis=0, concat_axis=0, tiled=True),
    )
    adapter_term = adapter_delta(
        landed_rows, landed_integers[:, 0], adapter_down_weight, adapter_up_weight
    )
    value_partial = project_input(landed_rows, query_key_value_weight, adapter_term)
    result = serve_rows(value_partial, landed_integers[:, 1], arrived_cache, cache_pos, keep_new)
    returned = lax.all_to_all(result, "replica", split_axis=0, concat_axis=0, tiled=True)
    return jnp.swapaxes(returned[slot_of], 0, 1)


def fold_columns(row, count):
    down = lax.broadcasted_iota(jnp.int32, (count, count), 0)
    along = lax.broadcasted_iota(jnp.int32, (count, count), 1)
    return jnp.sum(jnp.where(down == along, row, 0), axis=1, keepdims=True)


def gather_kernel(
    steps,
    hidden_hbm,
    weight_hbm,
    down_ref,
    up_ref,
    pool_hbm,
    home_ref,
    choice_ref,
    length_ref,
    table_ref,
    out_ref,
    hidden_v,
    weight_v,
    pool_v,
    pages_f32,
    pages,
    downs,
    ups,
    up_full,
    base,
    low,
    fresh_q,
    fresh_k,
    fresh_v,
    cosine,
    sine,
    local_sem,
    piece_send,
    piece_recv,
    up_send,
    up_recv,
    pair_send,
    pair_recv,
):
    rows, width = hidden_v.shape
    req = rows // steps
    head = base.shape[2] // 3
    half_block = pool_v.shape[1]
    entries = pool_v.shape[0]
    blocks = entries // req
    rank2 = downs.shape[2]
    rank = rank2 // 2
    g = lax.axis_index("groups")
    r = lax.axis_index("replica")
    t = lax.axis_index("tensor")
    z = r // 2
    x = r % 2
    far = {1: z + 1 - 2 * (z % 2), 2: (z + 2) % 4, 3: 3 - z}
    other_x = 1 - x
    z_dev = {d: {"replica": far[d] * 2 + x} for d in far}
    x_dev = {"replica": z * 2 + other_x}
    y_dev = {"groups": 1 - g}
    t_dev = {"tensor": 1 - t}

    barrier = pltpu.get_barrier_semaphore()
    for peer in (z_dev[1], z_dev[2], z_dev[3], x_dev, y_dev, t_dev):
        pl.semaphore_signal(barrier, inc=1, device_id=peer, device_id_type=pl.DeviceIdType.MESH)

    loads = [
        pltpu.make_async_copy(hidden_hbm, hidden_v, local_sem.at[0]),
        pltpu.make_async_copy(weight_hbm, weight_v, local_sem.at[1]),
        pltpu.make_async_copy(pool_hbm, pool_v, local_sem.at[2]),
    ]
    for load in loads:
        load.start()
    downs[r] = down_ref[...]
    ups[r] = up_ref[...]
    pl.semaphore_wait(barrier, 6)

    sent = []

    def piece(source, slot, device):
        index = len(sent) // 2
        return (
            pltpu.make_async_remote_copy(
                src_ref=downs.at[source, slot],
                dst_ref=downs.at[source, slot],
                send_sem=piece_send.at[index],
                recv_sem=piece_recv.at[source, slot],
                device_id=device,
                device_id_type=pl.DeviceIdType.MESH,
            ),
            pltpu.make_async_remote_copy(
                src_ref=ups.at[source, slot],
                dst_ref=ups.at[source, slot],
                send_sem=up_send.at[index],
                recv_sem=up_recv.at[source, slot],
                device_id=device,
                device_id_type=pl.DeviceIdType.MESH,
            ),
        )

    def send(source, slot, device):
        for copy in piece(source, slot, device):
            copy.start()
            sent.append(copy)

    def arrive(source, slot):
        for semaphores, buffer in ((piece_recv, downs), (up_recv, ups)):
            pltpu.make_async_copy(
                buffer.at[source, slot], buffer.at[source, slot], semaphores.at[source, slot]
            ).wait()

    def pair(source, target, index):
        copy = pltpu.make_async_remote_copy(
            src_ref=source,
            dst_ref=target,
            send_sem=pair_send.at[index],
            recv_sem=pair_recv.at[index],
            device_id=t_dev,
            device_id_type=pl.DeviceIdType.MESH,
        )
        copy.start()
        return copy

    ng = 1 - g
    near, mid, last = far[1] * 2, far[2] * 2, far[3] * 2
    here = z * 2

    send(r, g, x_dev)
    send(r, g, z_dev[1])
    send(r, g, z_dev[2])
    send(r, g, z_dev[3])
    send(r, ng, z_dev[1])

    loads[0].wait()
    loads[1].wait()
    base[0] = jnp.dot(hidden_v[...], weight_v[...], preferred_element_type=jnp.float32)
    base_copy = pair(base.at[0], base.at[1], 0)

    arrive(here + other_x, g)
    send(here + other_x, g, y_dev)
    arrive(near + x, g)
    send(near + x, g, x_dev)

    loads[2].wait()

    def take_page(entry, carry):
        page = pool_v[table_ref[0, entry]]
        pages_f32[pl.ds(pl.multiple_of(entry * half_block, half_block), half_block), :] = (
            page.astype(jnp.float32)
        )
        return carry

    third = entries // 3
    lax.fori_loop(0, third, take_page, 0, unroll=8)
    arrive(mid + x, g)
    send(mid + x, g, y_dev)
    send(mid + x, g, x_dev)
    lax.fori_loop(third, 2 * third, take_page, 0, unroll=8)
    arrive(last + x, g)
    send(last + x, g, y_dev)
    send(last + x, g, x_dev)
    lax.fori_loop(2 * third, entries, take_page, 0, unroll=8)
    pages[t] = pages_f32[...].astype(jnp.bfloat16)
    pages_copy = pair(pages.at[t], pages.at[t], 1)
    arrive(near + x, ng)
    send(near + x, ng, x_dev)

    length = fold_columns(length_ref[...], req)
    adapter = fold_columns(home_ref[...] * 2 + choice_ref[...], req)
    lengths = jnp.concatenate([length] * steps, axis=0)
    adapters = jnp.concatenate([adapter] * steps, axis=0)
    step_of = lax.broadcasted_iota(jnp.int32, (rows, 1), 0) // req
    position = (lengths + step_of).astype(jnp.float32)
    lane = lax.broadcasted_iota(jnp.int32, (1, head), 1)
    half = head // 2
    frequency = jnp.exp(
        (lane % half).astype(jnp.float32) * (-2.0 * math.log(rope_base) / head)
    )
    angles = position * frequency
    cosine[...] = jnp.cos(angles)
    sine[...] = jnp.where(lane < half, -jnp.sin(angles), jnp.sin(angles))

    def rotated(vector):
        turned = jnp.concatenate([vector[:, half:], vector[:, :half]], axis=1)
        return vector * cosine[...] + turned * sine[...]

    def rounded(vector):
        return vector.astype(jnp.bfloat16).astype(jnp.float32)

    def add_low(z_index, first):
        packed = downs[pl.ds(z_index * 2, 2)].reshape(4 * rank2, width)
        part = lax.dot_general(
            hidden_v[...], packed, (((1,), (1,)), ((), ())), preferred_element_type=jnp.float32
        )
        owner = lax.broadcasted_iota(jnp.int32, (1, 4 * rank2), 1) // rank2 + 4 * z_index
        part = jnp.where(adapters == owner, part, 0.0)
        low[0] = part if first else low[0] + part

    arrive(mid + other_x, g)
    send(mid + other_x, g, y_dev)
    base_copy.wait_recv()
    fresh_k[...] = rounded(rotated(base[0, :, head : 2 * head] + base[1, :, head : 2 * head]))
    arrive(last + other_x, g)
    send(last + other_x, g, y_dev)

    arrive(here + other_x, ng)
    add_low(z, True)
    arrive(near + other_x, g)
    arrive(near + other_x, ng)
    add_low(far[1], False)
    pages_copy.wait_recv()
    arrive(mid + x, ng)
    arrive(mid + other_x, ng)
    add_low(far[2], False)
    arrive(last + x, ng)
    arrive(last + other_x, ng)
    add_low(far[3], False)
    low_copy = pair(low.at[0], low.at[1], 2)

    up_full[...] = jnp.zeros_like(up_full)
    for source in range(ups.shape[0]):
        for slot in range(2):
            at = (source * 2 + slot) * rank2
            up_full[at : at + rank, :head] = ups[source, slot, :, :head]
            up_full[at + rank : at + rank2, head:] = ups[source, slot, :, head:]
    low_copy.wait_recv()

    low_sum = low[0] + low[1]
    count = up_full.shape[0]
    wide = jnp.concatenate([low_sum] * (count // (4 * rank2)), axis=1)
    owner = lax.broadcasted_iota(jnp.int32, (1, count), 1) // rank2
    wide = jnp.where(adapters == owner, wide, 0.0)
    high = wide.astype(jnp.bfloat16)
    rest = (wide - high.astype(jnp.float32)).astype(jnp.bfloat16)
    term = jnp.dot(high, up_full[...], preferred_element_type=jnp.float32) + jnp.dot(
        rest, up_full[...], preferred_element_type=jnp.float32
    )
    fresh_q[...] = rounded(rotated(base[0, :, :head] + base[1, :, :head] + term[:, :head]))
    fresh_v[...] = base[0, :, 2 * head :] + base[1, :, 2 * head :] + term[:, head:]

    each = 8
    local = steps * each
    span = each * blocks * half_block
    down_row = lax.broadcasted_iota(jnp.int32, (local, 1), 0)
    row_req = down_row % each
    row_step = down_row // each
    column = lax.broadcasted_iota(jnp.int32, (1, 2 * span), 1)
    side = column // span
    inner = column % span
    col_pos = (
        (inner // half_block) % blocks * (2 * half_block) + side * half_block + inner % half_block
    )
    same_old = inner // (blocks * half_block) == row_req
    new_col = lax.broadcasted_iota(jnp.int32, (1, local), 1)
    new_mask = (new_col % each == row_req) & (new_col // each <= row_step)
    scaling = 1.0 / math.sqrt(head)
    contract = (((1,), (1,)), ((), ()))

    for group in range(req // each):
        def picked(ref):
            return jnp.concatenate(
                [ref[s * req + group * each : s * req + (group + 1) * each, :] for s in range(steps)],
                axis=0,
            ).astype(jnp.bfloat16)

        limit = jnp.concatenate([length[group * each : (group + 1) * each]] * steps, axis=0)
        cached = jnp.concatenate(
            [pages[h, group * span : (group + 1) * span, :] for h in range(2)], axis=0
        )
        query, key, value = picked(fresh_q), picked(fresh_k), picked(fresh_v)
        old_mask = same_old & (col_pos < limit)
        old = lax.dot_general(
            query, cached[:, :head], contract, preferred_element_type=jnp.float32
        )
        new = lax.dot_general(query, key, contract, preferred_element_type=jnp.float32)
        old = jnp.where(old_mask, old * scaling, neg_fill)
        new = jnp.where(new_mask, new * scaling, neg_fill)
        peak = jnp.maximum(
            jnp.max(old, axis=1, keepdims=True), jnp.max(new, axis=1, keepdims=True)
        )
        old = jnp.where(old_mask, jnp.exp(old - peak), 0.0)
        new = jnp.where(new_mask, jnp.exp(new - peak), 0.0)
        total = jnp.sum(old, axis=1, keepdims=True) + jnp.sum(new, axis=1, keepdims=True)
        mixed = jnp.dot(
            old.astype(jnp.bfloat16), cached[:, head:], preferred_element_type=jnp.float32
        ) + jnp.dot(new.astype(jnp.bfloat16), value, preferred_element_type=jnp.float32)
        mixed = mixed / total
        for s in range(steps):
            out_ref[s, group * each : (group + 1) * each, :] = mixed[s * each : (s + 1) * each]

    for copy in sent + [base_copy, pages_copy, low_copy]:
        copy.wait_send()


def adapters_to_rows(
    hidden,
    query_key_value_weight,
    adapter_down_weight,
    adapter_up_weight,
    key_value_pool,
    adapter_replica,
    adapter_choice_index,
    cached_length,
    request_block_table,
):
    steps, req, width = hidden.shape
    held, rank, head2 = adapter_up_weight.shape
    head = head2 // 2
    _, entries, half_block, _ = key_value_pool.shape
    replicas = lax.axis_size("replica")
    rows = steps * req
    vmem = pl.BlockSpec(memory_space=pltpu.VMEM)
    hbm = pl.BlockSpec(memory_space=pl.ANY)
    smem = pl.BlockSpec(memory_space=pltpu.SMEM)
    sends = 14
    result = pl.pallas_call(
        functools.partial(gather_kernel, steps),
        out_shape=jax.ShapeDtypeStruct((steps, req, head), jnp.float32),
        in_specs=[hbm, hbm, vmem, vmem, hbm, vmem, vmem, vmem, smem],
        out_specs=vmem,
        scratch_shapes=[
            pltpu.VMEM((rows, width), hidden.dtype),
            pltpu.VMEM((width, 3 * head), query_key_value_weight.dtype),
            pltpu.VMEM((entries, half_block, head2), key_value_pool.dtype),
            pltpu.VMEM((entries * half_block, head2), jnp.float32),
            pltpu.VMEM((2, entries * half_block, head2), jnp.bfloat16),
            pltpu.VMEM((replicas, held, 2 * rank, width), jnp.bfloat16),
            pltpu.VMEM((replicas, held, rank, head2), jnp.bfloat16),
            pltpu.VMEM((replicas * held * 2 * rank, head2), jnp.bfloat16),
            pltpu.VMEM((2, rows, 3 * head), jnp.float32),
            pltpu.VMEM((2, rows, 8 * rank), jnp.float32),
            pltpu.VMEM((rows, head), jnp.float32),
            pltpu.VMEM((rows, head), jnp.float32),
            pltpu.VMEM((rows, head), jnp.float32),
            pltpu.VMEM((rows, head), jnp.float32),
            pltpu.VMEM((rows, head), jnp.float32),
            pltpu.SemaphoreType.DMA((3,)),
            pltpu.SemaphoreType.DMA((sends,)),
            pltpu.SemaphoreType.DMA((replicas, held)),
            pltpu.SemaphoreType.DMA((sends,)),
            pltpu.SemaphoreType.DMA((replicas, held)),
            pltpu.SemaphoreType.DMA((3,)),
            pltpu.SemaphoreType.DMA((3,)),
        ],
        compiler_params=pltpu.CompilerParams(
            collective_id=0, has_side_effects=True, vmem_limit_bytes=48 * 1024 * 1024
        ),
    )(
        hidden.reshape(rows, width),
        query_key_value_weight,
        jnp.swapaxes(adapter_down_weight, 1, 2),
        adapter_up_weight,
        key_value_pool[0],
        adapter_replica.reshape(1, req),
        adapter_choice_index.reshape(1, req),
        cached_length,
        request_block_table,
    )
    return result.astype(jnp.bfloat16)


def on_device(*arguments):
    fits = (
        lax.axis_size("replica") == 8
        and lax.axis_size("groups") == 2
        and lax.axis_size("tensor") == 2
        and arguments[3].shape[0] == 2
    )
    return (adapters_to_rows if fits else rows_to_adapters)(*arguments)


def solution(mesh):
    placed = (
        P(None, ("groups", "replica"), "tensor"),
        P("tensor", None),
        P("replica", "tensor", None),
        P("replica", None, None),
        P(("groups", "replica"), None, "tensor", None),
        P(("groups", "replica"), None),
        P(("groups", "replica")),
        P(("groups", "replica"), None),
        P(("groups", "replica"), None),
    )
    return jax.shard_map(
        on_device,
        mesh=mesh,
        in_specs=placed,
        out_specs=P(None, ("groups", "replica"), None),
        check_vma=False,
    )
```

```python
import functools
import math

import jax
import jax.numpy as jnp
from jax import lax
from jax.experimental import pallas as pl
from jax.experimental.pallas import tpu as pltpu
from jax.sharding import PartitionSpec as P

rope_base = 500000.0
neg_fill = -1e30


def combined_all(part, axis, combine):
    gathered = jax.tree.map(lambda a: lax.all_gather(a, axis), part)

    def take(source):
        return jax.tree.map(lambda a: lax.dynamic_index_in_dim(a, source, 0, False), gathered)

    return lax.fori_loop(
        1, lax.axis_size(axis), lambda source, state: combine(state, take(source)), take(0)
    )


def rotate(vector, position):
    half_len = vector.shape[-1] // 2
    frequency = rope_base ** (-(jnp.arange(half_len, dtype=jnp.float32) * 2.0) / vector.shape[-1])
    angles = position[..., None].astype(jnp.float32) * frequency
    cosine = jnp.cos(angles)
    sine_part = jnp.sin(angles)
    first_part = vector[..., :half_len]
    second = vector[..., half_len:]
    return jnp.concatenate(
        [first_part * cosine - second * sine_part, second * cosine + first_part * sine_part],
        axis=-1,
    )


def adapter_delta(row_payload, choice_index, adapter_down_weight, adapter_up_weight):
    req_count, step_count, feat_width = row_payload.shape
    adapter_rank_width = adapter_up_weight.shape[1]
    head_width = adapter_up_weight.shape[2] // 2
    flattened_rows = row_payload.reshape(req_count * step_count, feat_width)
    summed = jnp.zeros((req_count, step_count, 2 * head_width), jnp.float32)
    highest_precision = lax.Precision.HIGHEST
    for adapter_slot in range(adapter_down_weight.shape[0]):
        reduced_rank = jnp.dot(
            flattened_rows, adapter_down_weight[adapter_slot], preferred_element_type=jnp.float32
        ).reshape(req_count, step_count, 2 * adapter_rank_width)
        up_matrix = adapter_up_weight[adapter_slot].astype(jnp.float32)
        query_term = jnp.einsum(
            "nsr,re->nse",
            reduced_rank[..., :adapter_rank_width],
            up_matrix[:, :head_width],
            precision=highest_precision,
        )
        value_term = jnp.einsum(
            "nsr,re->nse",
            reduced_rank[..., adapter_rank_width:],
            up_matrix[:, head_width:],
            precision=highest_precision,
        )
        chosen = (choice_index == adapter_slot)[:, None, None]
        summed = summed + jnp.where(chosen, jnp.concatenate([query_term, value_term], axis=-1), 0.0)
    return summed


def project_input(row_payload, query_key_value_weight, adapter_term):
    req_count, step_count, feat_width = row_payload.shape
    base_part = jnp.dot(
        row_payload.reshape(req_count * step_count, feat_width),
        query_key_value_weight,
        preferred_element_type=jnp.float32,
    ).reshape(req_count, step_count, -1)
    head_width = adapter_term.shape[-1] // 2
    middle_zeros = jnp.zeros(adapter_term.shape[:-1] + (head_width,), jnp.float32)
    return base_part + jnp.concatenate(
        [adapter_term[..., :head_width], middle_zeros, adapter_term[..., head_width:]], axis=-1
    )


def attend(summed, seq_lens, cached, cache_pos, keep_new):
    head_width = cached.shape[-1] // 2
    step_count = summed.shape[1]
    step_ids = jnp.arange(step_count, dtype=jnp.int32)
    position = seq_lens[:, None] + step_ids[None, :]
    queries = rotate(summed[..., :head_width], position).astype(jnp.bfloat16)
    fresh_k = rotate(summed[..., head_width : 2 * head_width], position).astype(jnp.bfloat16)
    fresh_v = summed[..., 2 * head_width :].astype(jnp.bfloat16)
    scaling = 1.0 / math.sqrt(head_width)
    old_scores = (
        jnp.einsum(
            "nsh,nph->nsp", queries, cached[..., :head_width], preferred_element_type=jnp.float32
        )
        * scaling
    )
    new_scores = (
        jnp.einsum("nsh,nth->nst", queries, fresh_k, preferred_element_type=jnp.float32) * scaling
    )
    old_mask = jnp.broadcast_to(
        cache_pos[None, None, :] < seq_lens[:, None, None], old_scores.shape
    )
    new_mask = jnp.broadcast_to(
        (step_ids[None, :, None] >= step_ids[None, None, :]) & keep_new, new_scores.shape
    )
    old_scores = jnp.where(old_mask, old_scores, neg_fill)
    new_scores = jnp.where(new_mask, new_scores, neg_fill)
    peak_val = jnp.maximum(jnp.max(old_scores, axis=-1), jnp.max(new_scores, axis=-1))
    old_exp = jnp.where(old_mask, jnp.exp(old_scores - peak_val[..., None]), 0.0)
    new_exp = jnp.where(new_mask, jnp.exp(new_scores - peak_val[..., None]), 0.0)
    total_sum = jnp.sum(old_exp, axis=-1) + jnp.sum(new_exp, axis=-1)
    accum = jnp.einsum(
        "nsp,nph->nsh",
        old_exp.astype(jnp.bfloat16),
        cached[..., head_width:],
        preferred_element_type=jnp.float32,
    )
    accum = accum + jnp.einsum(
        "nst,nth->nsh", new_exp.astype(jnp.bfloat16), fresh_v, preferred_element_type=jnp.float32
    )
    return (peak_val, total_sum, accum)


def combine(first_part, second):
    peak_val = jnp.maximum(first_part[0], second[0])
    left_scale = jnp.exp(first_part[0] - peak_val)
    right_scale = jnp.exp(second[0] - peak_val)
    return (
        peak_val,
        first_part[1] * left_scale + second[1] * right_scale,
        first_part[2] * left_scale[..., None] + second[2] * right_scale[..., None],
    )


def serve_rows(value_partial, seq_lens, cached, cache_pos, keep_new):
    summed = lax.psum(value_partial, "tensor")
    stats = attend(summed, seq_lens, cached, cache_pos, keep_new)
    peak_val, total_sum, accum = combined_all(stats, "tensor", combine)
    return (accum / total_sum[..., None]).astype(jnp.bfloat16)


def rows_to_adapters(
    hidden,
    query_key_value_weight,
    adapter_down_weight,
    adapter_up_weight,
    key_value_pool,
    adapter_replica,
    adapter_choice_index,
    cached_length,
    request_block_table,
):
    step_count, req_count, feat_width = hidden.shape
    half_len = key_value_pool.shape[2]
    head_width = key_value_pool.shape[3] // 2
    blocks = request_block_table.shape[1] // req_count
    replica_count = lax.axis_size("replica")
    slot_cap = max(2, (2 * req_count + replica_count - 1) // replica_count)
    tensor_id = lax.axis_index("tensor")
    keep_new = tensor_id == 0
    cache_pos = (
        jnp.arange(blocks, dtype=jnp.int32)[:, None] * (half_len * lax.axis_size("tensor"))
        + tensor_id * half_len
        + jnp.arange(half_len, dtype=jnp.int32)[None, :]
    ).reshape(-1)
    seq_lens = cached_length[0]
    home_rep = adapter_replica[:, 0]
    order_idx = jnp.arange(req_count, dtype=jnp.int32)
    earlier = (home_rep[:, None] == home_rep[None, :]) & (order_idx[None, :] < order_idx[:, None])
    slot_of = home_rep * slot_cap + jnp.sum(earlier.astype(jnp.int32), axis=1)
    slot_total = replica_count * slot_cap
    local_rows = jnp.swapaxes(hidden, 0, 1)
    row_buffer = (
        jnp.zeros((slot_total, step_count, feat_width), hidden.dtype).at[slot_of].set(local_rows)
    )
    cached = key_value_pool[0][request_block_table[0].reshape(req_count, blocks)].reshape(
        req_count, blocks * half_len, 2 * head_width
    )
    cache_buffer = (
        jnp.zeros((slot_total, blocks * half_len, 2 * head_width), key_value_pool.dtype)
        .at[slot_of]
        .set(cached)
    )
    meta_ints = (
        jnp.zeros((slot_total, 2), jnp.int32)
        .at[slot_of]
        .set(jnp.stack([adapter_choice_index, seq_lens], axis=1))
    )
    landed_rows, arrived_cache, landed_integers = (
        lax.all_to_all(row_buffer, "replica", split_axis=0, concat_axis=0, tiled=True),
        lax.all_to_all(cache_buffer, "replica", split_axis=0, concat_axis=0, tiled=True),
        lax.all_to_all(meta_ints, "replica", split_axis=0, concat_axis=0, tiled=True),
    )
    adapter_term = adapter_delta(
        landed_rows, landed_integers[:, 0], adapter_down_weight, adapter_up_weight
    )
    value_partial = project_input(landed_rows, query_key_value_weight, adapter_term)
    result = serve_rows(value_partial, landed_integers[:, 1], arrived_cache, cache_pos, keep_new)
    returned = lax.all_to_all(result, "replica", split_axis=0, concat_axis=0, tiled=True)
    return jnp.swapaxes(returned[slot_of], 0, 1)


def fold_columns(row, count):
    down = lax.broadcasted_iota(jnp.int32, (count, count), 0)
    along = lax.broadcasted_iota(jnp.int32, (count, count), 1)
    return jnp.sum(jnp.where(down == along, row, 0), axis=1, keepdims=True)


def gather_kernel(
    steps,
    hidden_hbm,
    weight_hbm,
    down_hbm,
    up_hbm,
    pool_hbm,
    home_hbm,
    choice_hbm,
    length_hbm,
    table_hbm,
    out_ref,
    hidden_v,
    weight_v,
    pool_v,
    home_ref,
    choice_ref,
    length_ref,
    table_ref,
    pages_f32,
    pages,
    downs,
    ups,
    up_full,
    base,
    low,
    fresh_q,
    fresh_k,
    fresh_v,
    cosine,
    sine,
    local_sem,
    piece_send,
    piece_recv,
    up_send,
    up_recv,
    pair_send,
    pair_recv,
):
    rows, width = hidden_v.shape
    req = rows // steps
    head = base.shape[2] // 3
    half_block = pool_v.shape[1]
    entries = pool_v.shape[0]
    blocks = entries // req
    rank2 = downs.shape[2]
    rank = rank2 // 2
    g = lax.axis_index("groups")
    r = lax.axis_index("replica")
    t = lax.axis_index("tensor")
    z = r // 2
    x = r % 2
    far = {1: z + 1 - 2 * (z % 2), 2: (z + 2) % 4, 3: 3 - z}
    other_x = 1 - x
    z_dev = {d: {"replica": far[d] * 2 + x} for d in far}
    x_dev = {"replica": z * 2 + other_x}
    y_dev = {"groups": 1 - g}
    t_dev = {"tensor": 1 - t}

    barrier = pltpu.get_barrier_semaphore()
    for peer in (z_dev[1], z_dev[2], z_dev[3], x_dev, y_dev, t_dev):
        pl.semaphore_signal(barrier, inc=1, device_id=peer, device_id_type=pl.DeviceIdType.MESH)

    own = (
        (down_hbm, downs.at[r]),
        (up_hbm, ups.at[r]),
        (hidden_hbm, hidden_v),
        (weight_hbm, weight_v),
        (pool_hbm, pool_v),
        (table_hbm, table_ref),
        (length_hbm, length_ref),
        (home_hbm, home_ref),
        (choice_hbm, choice_ref),
    )
    loads = [
        pltpu.make_async_copy(source, target, local_sem.at[index])
        for index, (source, target) in enumerate(own)
    ]
    for load in loads:
        load.start()
    loads[0].wait()
    loads[1].wait()
    pl.semaphore_wait(barrier, 6)

    sent = []

    def piece(source, slot, device):
        index = len(sent) // 2
        return (
            pltpu.make_async_remote_copy(
                src_ref=downs.at[source, slot],
                dst_ref=downs.at[source, slot],
                send_sem=piece_send.at[index],
                recv_sem=piece_recv.at[source, slot],
                device_id=device,
                device_id_type=pl.DeviceIdType.MESH,
            ),
            pltpu.make_async_remote_copy(
                src_ref=ups.at[source, slot],
                dst_ref=ups.at[source, slot],
                send_sem=up_send.at[index],
                recv_sem=up_recv.at[source, slot],
                device_id=device,
                device_id_type=pl.DeviceIdType.MESH,
            ),
        )

    def send(source, slot, device):
        for copy in piece(source, slot, device):
            copy.start()
            sent.append(copy)

    def arrive(source, slot):
        for semaphores, buffer in ((piece_recv, downs), (up_recv, ups)):
            pltpu.make_async_copy(
                buffer.at[source, slot], buffer.at[source, slot], semaphores.at[source, slot]
            ).wait()

    def pair(source, target, index):
        copy = pltpu.make_async_remote_copy(
            src_ref=source,
            dst_ref=target,
            send_sem=pair_send.at[index],
            recv_sem=pair_recv.at[index],
            device_id=t_dev,
            device_id_type=pl.DeviceIdType.MESH,
        )
        copy.start()
        return copy

    ng = 1 - g
    near, mid, last = far[1] * 2, far[2] * 2, far[3] * 2
    here = z * 2

    send(r, g, x_dev)
    send(r, g, z_dev[1])
    send(r, g, z_dev[2])
    send(r, g, z_dev[3])
    send(r, ng, z_dev[1])

    loads[2].wait()
    loads[3].wait()
    base[0] = jnp.dot(hidden_v[...], weight_v[...], preferred_element_type=jnp.float32)
    base_copy = pair(base.at[0], base.at[1], 0)

    arrive(here + other_x, g)
    send(here + other_x, g, y_dev)
    arrive(near + x, g)
    send(near + x, g, x_dev)

    for load in loads[4:]:
        load.wait()

    def take_page(entry, carry):
        page = pool_v[table_ref[0, entry]]
        pages_f32[pl.ds(pl.multiple_of(entry * half_block, half_block), half_block), :] = (
            page.astype(jnp.float32)
        )
        return carry

    third = entries // 3
    lax.fori_loop(0, third, take_page, 0, unroll=8)
    arrive(mid + x, g)
    send(mid + x, g, y_dev)
    send(mid + x, g, x_dev)
    lax.fori_loop(third, 2 * third, take_page, 0, unroll=8)
    arrive(last + x, g)
    send(last + x, g, y_dev)
    send(last + x, g, x_dev)
    lax.fori_loop(2 * third, entries, take_page, 0, unroll=8)
    pages[t] = pages_f32[...].astype(jnp.bfloat16)
    pages_copy = pair(pages.at[t], pages.at[t], 1)
    arrive(near + x, ng)
    send(near + x, ng, x_dev)

    length = fold_columns(length_ref[...], req)
    adapter = fold_columns(home_ref[...] * 2 + choice_ref[...], req)
    lengths = jnp.concatenate([length] * steps, axis=0)
    adapters = jnp.concatenate([adapter] * steps, axis=0)
    step_of = lax.broadcasted_iota(jnp.int32, (rows, 1), 0) // req
    position = (lengths + step_of).astype(jnp.float32)
    lane = lax.broadcasted_iota(jnp.int32, (1, head), 1)
    half = head // 2
    frequency = jnp.exp(
        (lane % half).astype(jnp.float32) * (-2.0 * math.log(rope_base) / head)
    )
    angles = position * frequency
    cosine[...] = jnp.cos(angles)
    sine[...] = jnp.where(lane < half, -jnp.sin(angles), jnp.sin(angles))

    def rotated(vector):
        turned = jnp.concatenate([vector[:, half:], vector[:, :half]], axis=1)
        return vector * cosine[...] + turned * sine[...]

    def rounded(vector):
        return vector.astype(jnp.bfloat16).astype(jnp.float32)

    def add_low(z_index, first):
        packed = downs[pl.ds(z_index * 2, 2)].reshape(4 * rank2, width)
        part = lax.dot_general(
            hidden_v[...], packed, (((1,), (1,)), ((), ())), preferred_element_type=jnp.float32
        )
        owner = lax.broadcasted_iota(jnp.int32, (1, 4 * rank2), 1) // rank2 + 4 * z_index
        part = jnp.where(adapters == owner, part, 0.0)
        low[0] = part if first else low[0] + part

    arrive(mid + other_x, g)
    send(mid + other_x, g, y_dev)
    base_copy.wait_recv()
    fresh_k[...] = rounded(rotated(base[0, :, head : 2 * head] + base[1, :, head : 2 * head]))
    arrive(last + other_x, g)
    send(last + other_x, g, y_dev)

    arrive(here + other_x, ng)
    add_low(z, True)
    arrive(near + other_x, g)
    arrive(near + other_x, ng)
    add_low(far[1], False)
    pages_copy.wait_recv()
    arrive(mid + x, ng)
    arrive(mid + other_x, ng)
    add_low(far[2], False)
    arrive(last + x, ng)
    arrive(last + other_x, ng)
    add_low(far[3], False)
    low_copy = pair(low.at[0], low.at[1], 2)

    up_full[...] = jnp.zeros_like(up_full)
    for source in range(ups.shape[0]):
        for slot in range(2):
            at = (source * 2 + slot) * rank2
            up_full[at : at + rank, :head] = ups[source, slot, :, :head]
            up_full[at + rank : at + rank2, head:] = ups[source, slot, :, head:]
    low_copy.wait_recv()

    low_sum = low[0] + low[1]
    count = up_full.shape[0]
    wide = jnp.concatenate([low_sum] * (count // (4 * rank2)), axis=1)
    owner = lax.broadcasted_iota(jnp.int32, (1, count), 1) // rank2
    wide = jnp.where(adapters == owner, wide, 0.0)
    high = wide.astype(jnp.bfloat16)
    rest = (wide - high.astype(jnp.float32)).astype(jnp.bfloat16)
    term = jnp.dot(high, up_full[...], preferred_element_type=jnp.float32) + jnp.dot(
        rest, up_full[...], preferred_element_type=jnp.float32
    )
    fresh_q[...] = rounded(rotated(base[0, :, :head] + base[1, :, :head] + term[:, :head]))
    fresh_v[...] = base[0, :, 2 * head :] + base[1, :, 2 * head :] + term[:, head:]

    each = 8
    local = steps * each
    span = each * blocks * half_block
    down_row = lax.broadcasted_iota(jnp.int32, (local, 1), 0)
    row_req = down_row % each
    row_step = down_row // each
    column = lax.broadcasted_iota(jnp.int32, (1, 2 * span), 1)
    side = column // span
    inner = column % span
    col_pos = (
        (inner // half_block) % blocks * (2 * half_block) + side * half_block + inner % half_block
    )
    same_old = inner // (blocks * half_block) == row_req
    new_col = lax.broadcasted_iota(jnp.int32, (1, local), 1)
    new_mask = (new_col % each == row_req) & (new_col // each <= row_step)
    scaling = 1.0 / math.sqrt(head)
    contract = (((1,), (1,)), ((), ()))

    for group in range(req // each):
        def picked(ref):
            return jnp.concatenate(
                [ref[s * req + group * each : s * req + (group + 1) * each, :] for s in range(steps)],
                axis=0,
            ).astype(jnp.bfloat16)

        limit = jnp.concatenate([length[group * each : (group + 1) * each]] * steps, axis=0)
        cached = jnp.concatenate(
            [pages[h, group * span : (group + 1) * span, :] for h in range(2)], axis=0
        )
        query, key, value = picked(fresh_q), picked(fresh_k), picked(fresh_v)
        old_mask = same_old & (col_pos < limit)
        old = lax.dot_general(
            query, cached[:, :head], contract, preferred_element_type=jnp.float32
        )
        new = lax.dot_general(query, key, contract, preferred_element_type=jnp.float32)
        old = jnp.where(old_mask, old * scaling, neg_fill)
        new = jnp.where(new_mask, new * scaling, neg_fill)
        peak = jnp.maximum(
            jnp.max(old, axis=1, keepdims=True), jnp.max(new, axis=1, keepdims=True)
        )
        old = jnp.where(old_mask, jnp.exp(old - peak), 0.0)
        new = jnp.where(new_mask, jnp.exp(new - peak), 0.0)
        total = jnp.sum(old, axis=1, keepdims=True) + jnp.sum(new, axis=1, keepdims=True)
        mixed = jnp.dot(
            old.astype(jnp.bfloat16), cached[:, head:], preferred_element_type=jnp.float32
        ) + jnp.dot(new.astype(jnp.bfloat16), value, preferred_element_type=jnp.float32)
        mixed = mixed / total
        for s in range(steps):
            out_ref[s, group * each : (group + 1) * each, :] = mixed[s * each : (s + 1) * each]

    for copy in sent + [base_copy, pages_copy, low_copy]:
        copy.wait_send()


def adapters_to_rows(
    hidden,
    query_key_value_weight,
    adapter_down_weight,
    adapter_up_weight,
    key_value_pool,
    adapter_replica,
    adapter_choice_index,
    cached_length,
    request_block_table,
):
    steps, req, width = hidden.shape
    held, rank, head2 = adapter_up_weight.shape
    head = head2 // 2
    _, entries, half_block, _ = key_value_pool.shape
    replicas = lax.axis_size("replica")
    rows = steps * req
    vmem = pl.BlockSpec(memory_space=pltpu.VMEM)
    hbm = pl.BlockSpec(memory_space=pltpu.HBM)
    sends = 14
    result = pl.pallas_call(
        functools.partial(gather_kernel, steps),
        out_shape=jax.ShapeDtypeStruct((steps, req, head), jnp.float32),
        in_specs=[hbm] * 9,
        out_specs=vmem,
        scratch_shapes=[
            pltpu.VMEM((rows, width), hidden.dtype),
            pltpu.VMEM((width, 3 * head), query_key_value_weight.dtype),
            pltpu.VMEM((entries, half_block, head2), key_value_pool.dtype),
            pltpu.VMEM((1, req), jnp.int32),
            pltpu.VMEM((1, req), jnp.int32),
            pltpu.VMEM((1, req), jnp.int32),
            pltpu.SMEM((1, entries), jnp.int32),
            pltpu.VMEM((entries * half_block, head2), jnp.float32),
            pltpu.VMEM((2, entries * half_block, head2), jnp.bfloat16),
            pltpu.VMEM((replicas, held, 2 * rank, width), jnp.bfloat16),
            pltpu.VMEM((replicas, held, rank, head2), jnp.bfloat16),
            pltpu.VMEM((replicas * held * 2 * rank, head2), jnp.bfloat16),
            pltpu.VMEM((2, rows, 3 * head), jnp.float32),
            pltpu.VMEM((2, rows, 8 * rank), jnp.float32),
            pltpu.VMEM((rows, head), jnp.float32),
            pltpu.VMEM((rows, head), jnp.float32),
            pltpu.VMEM((rows, head), jnp.float32),
            pltpu.VMEM((rows, head), jnp.float32),
            pltpu.VMEM((rows, head), jnp.float32),
            pltpu.SemaphoreType.DMA((9,)),
            pltpu.SemaphoreType.DMA((sends,)),
            pltpu.SemaphoreType.DMA((replicas, held)),
            pltpu.SemaphoreType.DMA((sends,)),
            pltpu.SemaphoreType.DMA((replicas, held)),
            pltpu.SemaphoreType.DMA((3,)),
            pltpu.SemaphoreType.DMA((3,)),
        ],
        compiler_params=pltpu.CompilerParams(
            collective_id=0, has_side_effects=True, vmem_limit_bytes=64 * 1024 * 1024
        ),
    )(
        hidden.reshape(rows, width),
        query_key_value_weight,
        jnp.swapaxes(adapter_down_weight, 1, 2),
        adapter_up_weight,
        key_value_pool[0],
        adapter_replica.reshape(1, req),
        adapter_choice_index.reshape(1, req),
        cached_length,
        request_block_table,
    )
    return result.astype(jnp.bfloat16)


def on_device(*arguments):
    fits = (
        lax.axis_size("replica") == 8
        and lax.axis_size("groups") == 2
        and lax.axis_size("tensor") == 2
        and arguments[3].shape[0] == 2
    )
    return (adapters_to_rows if fits else rows_to_adapters)(*arguments)


def solution(mesh):
    placed = (
        P(None, ("groups", "replica"), "tensor"),
        P("tensor", None),
        P("replica", "tensor", None),
        P("replica", None, None),
        P(("groups", "replica"), None, "tensor", None),
        P(("groups", "replica"), None),
        P(("groups", "replica")),
        P(("groups", "replica"), None),
        P(("groups", "replica"), None),
    )
    return jax.shard_map(
        on_device,
        mesh=mesh,
        in_specs=placed,
        out_specs=P(None, ("groups", "replica"), None),
        check_vma=False,
    )
```

```python
import functools
import math

import jax
import jax.numpy as jnp
from jax import lax
from jax.experimental import pallas as pl
from jax.experimental.pallas import tpu as pltpu
from jax.sharding import PartitionSpec as P

rope_base = 500000.0
neg_fill = -1e30


def combined_all(part, axis, combine):
    gathered = jax.tree.map(lambda a: lax.all_gather(a, axis), part)

    def take(source):
        return jax.tree.map(lambda a: lax.dynamic_index_in_dim(a, source, 0, False), gathered)

    return lax.fori_loop(
        1, lax.axis_size(axis), lambda source, state: combine(state, take(source)), take(0)
    )


def rotate(vector, position):
    half_len = vector.shape[-1] // 2
    frequency = rope_base ** (-(jnp.arange(half_len, dtype=jnp.float32) * 2.0) / vector.shape[-1])
    angles = position[..., None].astype(jnp.float32) * frequency
    cosine = jnp.cos(angles)
    sine_part = jnp.sin(angles)
    first_part = vector[..., :half_len]
    second = vector[..., half_len:]
    return jnp.concatenate(
        [first_part * cosine - second * sine_part, second * cosine + first_part * sine_part],
        axis=-1,
    )


def adapter_delta(row_payload, choice_index, adapter_down_weight, adapter_up_weight):
    req_count, step_count, feat_width = row_payload.shape
    adapter_rank_width = adapter_up_weight.shape[1]
    head_width = adapter_up_weight.shape[2] // 2
    flattened_rows = row_payload.reshape(req_count * step_count, feat_width)
    summed = jnp.zeros((req_count, step_count, 2 * head_width), jnp.float32)
    highest_precision = lax.Precision.HIGHEST
    for adapter_slot in range(adapter_down_weight.shape[0]):
        reduced_rank = jnp.dot(
            flattened_rows, adapter_down_weight[adapter_slot], preferred_element_type=jnp.float32
        ).reshape(req_count, step_count, 2 * adapter_rank_width)
        up_matrix = adapter_up_weight[adapter_slot].astype(jnp.float32)
        query_term = jnp.einsum(
            "nsr,re->nse",
            reduced_rank[..., :adapter_rank_width],
            up_matrix[:, :head_width],
            precision=highest_precision,
        )
        value_term = jnp.einsum(
            "nsr,re->nse",
            reduced_rank[..., adapter_rank_width:],
            up_matrix[:, head_width:],
            precision=highest_precision,
        )
        chosen = (choice_index == adapter_slot)[:, None, None]
        summed = summed + jnp.where(chosen, jnp.concatenate([query_term, value_term], axis=-1), 0.0)
    return summed


def project_input(row_payload, query_key_value_weight, adapter_term):
    req_count, step_count, feat_width = row_payload.shape
    base_part = jnp.dot(
        row_payload.reshape(req_count * step_count, feat_width),
        query_key_value_weight,
        preferred_element_type=jnp.float32,
    ).reshape(req_count, step_count, -1)
    head_width = adapter_term.shape[-1] // 2
    middle_zeros = jnp.zeros(adapter_term.shape[:-1] + (head_width,), jnp.float32)
    return base_part + jnp.concatenate(
        [adapter_term[..., :head_width], middle_zeros, adapter_term[..., head_width:]], axis=-1
    )


def attend(summed, seq_lens, cached, cache_pos, keep_new):
    head_width = cached.shape[-1] // 2
    step_count = summed.shape[1]
    step_ids = jnp.arange(step_count, dtype=jnp.int32)
    position = seq_lens[:, None] + step_ids[None, :]
    queries = rotate(summed[..., :head_width], position).astype(jnp.bfloat16)
    fresh_k = rotate(summed[..., head_width : 2 * head_width], position).astype(jnp.bfloat16)
    fresh_v = summed[..., 2 * head_width :].astype(jnp.bfloat16)
    scaling = 1.0 / math.sqrt(head_width)
    old_scores = (
        jnp.einsum(
            "nsh,nph->nsp", queries, cached[..., :head_width], preferred_element_type=jnp.float32
        )
        * scaling
    )
    new_scores = (
        jnp.einsum("nsh,nth->nst", queries, fresh_k, preferred_element_type=jnp.float32) * scaling
    )
    old_mask = jnp.broadcast_to(
        cache_pos[None, None, :] < seq_lens[:, None, None], old_scores.shape
    )
    new_mask = jnp.broadcast_to(
        (step_ids[None, :, None] >= step_ids[None, None, :]) & keep_new, new_scores.shape
    )
    old_scores = jnp.where(old_mask, old_scores, neg_fill)
    new_scores = jnp.where(new_mask, new_scores, neg_fill)
    peak_val = jnp.maximum(jnp.max(old_scores, axis=-1), jnp.max(new_scores, axis=-1))
    old_exp = jnp.where(old_mask, jnp.exp(old_scores - peak_val[..., None]), 0.0)
    new_exp = jnp.where(new_mask, jnp.exp(new_scores - peak_val[..., None]), 0.0)
    total_sum = jnp.sum(old_exp, axis=-1) + jnp.sum(new_exp, axis=-1)
    accum = jnp.einsum(
        "nsp,nph->nsh",
        old_exp.astype(jnp.bfloat16),
        cached[..., head_width:],
        preferred_element_type=jnp.float32,
    )
    accum = accum + jnp.einsum(
        "nst,nth->nsh", new_exp.astype(jnp.bfloat16), fresh_v, preferred_element_type=jnp.float32
    )
    return (peak_val, total_sum, accum)


def combine(first_part, second):
    peak_val = jnp.maximum(first_part[0], second[0])
    left_scale = jnp.exp(first_part[0] - peak_val)
    right_scale = jnp.exp(second[0] - peak_val)
    return (
        peak_val,
        first_part[1] * left_scale + second[1] * right_scale,
        first_part[2] * left_scale[..., None] + second[2] * right_scale[..., None],
    )


def serve_rows(value_partial, seq_lens, cached, cache_pos, keep_new):
    summed = lax.psum(value_partial, "tensor")
    stats = attend(summed, seq_lens, cached, cache_pos, keep_new)
    peak_val, total_sum, accum = combined_all(stats, "tensor", combine)
    return (accum / total_sum[..., None]).astype(jnp.bfloat16)


def rows_to_adapters(
    hidden,
    query_key_value_weight,
    adapter_down_weight,
    adapter_up_weight,
    key_value_pool,
    adapter_replica,
    adapter_choice_index,
    cached_length,
    request_block_table,
):
    step_count, req_count, feat_width = hidden.shape
    half_len = key_value_pool.shape[2]
    head_width = key_value_pool.shape[3] // 2
    blocks = request_block_table.shape[1] // req_count
    replica_count = lax.axis_size("replica")
    slot_cap = max(2, (2 * req_count + replica_count - 1) // replica_count)
    tensor_id = lax.axis_index("tensor")
    keep_new = tensor_id == 0
    cache_pos = (
        jnp.arange(blocks, dtype=jnp.int32)[:, None] * (half_len * lax.axis_size("tensor"))
        + tensor_id * half_len
        + jnp.arange(half_len, dtype=jnp.int32)[None, :]
    ).reshape(-1)
    seq_lens = cached_length[0]
    home_rep = adapter_replica[:, 0]
    order_idx = jnp.arange(req_count, dtype=jnp.int32)
    earlier = (home_rep[:, None] == home_rep[None, :]) & (order_idx[None, :] < order_idx[:, None])
    slot_of = home_rep * slot_cap + jnp.sum(earlier.astype(jnp.int32), axis=1)
    slot_total = replica_count * slot_cap
    local_rows = jnp.swapaxes(hidden, 0, 1)
    row_buffer = (
        jnp.zeros((slot_total, step_count, feat_width), hidden.dtype).at[slot_of].set(local_rows)
    )
    cached = key_value_pool[0][request_block_table[0].reshape(req_count, blocks)].reshape(
        req_count, blocks * half_len, 2 * head_width
    )
    cache_buffer = (
        jnp.zeros((slot_total, blocks * half_len, 2 * head_width), key_value_pool.dtype)
        .at[slot_of]
        .set(cached)
    )
    meta_ints = (
        jnp.zeros((slot_total, 2), jnp.int32)
        .at[slot_of]
        .set(jnp.stack([adapter_choice_index, seq_lens], axis=1))
    )
    landed_rows, arrived_cache, landed_integers = (
        lax.all_to_all(row_buffer, "replica", split_axis=0, concat_axis=0, tiled=True),
        lax.all_to_all(cache_buffer, "replica", split_axis=0, concat_axis=0, tiled=True),
        lax.all_to_all(meta_ints, "replica", split_axis=0, concat_axis=0, tiled=True),
    )
    adapter_term = adapter_delta(
        landed_rows, landed_integers[:, 0], adapter_down_weight, adapter_up_weight
    )
    value_partial = project_input(landed_rows, query_key_value_weight, adapter_term)
    result = serve_rows(value_partial, landed_integers[:, 1], arrived_cache, cache_pos, keep_new)
    returned = lax.all_to_all(result, "replica", split_axis=0, concat_axis=0, tiled=True)
    return jnp.swapaxes(returned[slot_of], 0, 1)


def fold_columns(row, count):
    down = lax.broadcasted_iota(jnp.int32, (count, count), 0)
    along = lax.broadcasted_iota(jnp.int32, (count, count), 1)
    return jnp.sum(jnp.where(down == along, row, 0), axis=1, keepdims=True)


def gather_kernel(
    steps,
    hidden_hbm,
    weight_hbm,
    down_hbm,
    up_hbm,
    pool_hbm,
    home_hbm,
    choice_hbm,
    length_hbm,
    table_hbm,
    out_ref,
    hidden_v,
    weight_v,
    pool_v,
    home_ref,
    choice_ref,
    length_ref,
    table_ref,
    pages_f32,
    pages,
    downs,
    ups,
    up_full,
    base,
    low,
    hidden_y,
    names,
    packed_low,
    fresh_q,
    fresh_k,
    fresh_v,
    cosine,
    sine,
    local_sem,
    piece_send,
    piece_recv,
    up_send,
    up_recv,
    pair_send,
    pair_recv,
    cross_send,
    cross_recv,
):
    rows, width = hidden_v.shape
    req = rows // steps
    head = base.shape[2] // 3
    half_block = pool_v.shape[1]
    entries = pool_v.shape[0]
    blocks = entries // req
    rank2 = downs.shape[2]
    rank = rank2 // 2
    g = lax.axis_index("groups")
    r = lax.axis_index("replica")
    t = lax.axis_index("tensor")
    z = r // 2
    x = r % 2
    far = {1: z + 1 - 2 * (z % 2), 2: (z + 2) % 4, 3: 3 - z}
    other_x = 1 - x
    z_dev = {d: {"replica": far[d] * 2 + x} for d in far}
    x_dev = {"replica": z * 2 + other_x}
    y_dev = {"groups": 1 - g}
    t_dev = {"tensor": 1 - t}
    yt_dev = {"groups": 1 - g, "tensor": 1 - t}
    part_width = width // 2
    mine = pl.ds(pl.multiple_of(g * part_width, part_width), part_width)
    theirs = pl.ds(pl.multiple_of((1 - g) * part_width, part_width), part_width)

    barrier = pltpu.get_barrier_semaphore()
    for peer in (z_dev[1], z_dev[2], z_dev[3], x_dev, y_dev, t_dev, yt_dev):
        pl.semaphore_signal(barrier, inc=1, device_id=peer, device_id_type=pl.DeviceIdType.MESH)

    own = (
        (down_hbm.at[:, :, mine], downs.at[r]),
        (up_hbm.at[t], ups.at[t, r]),
        (hidden_hbm, hidden_v),
        (weight_hbm, weight_v),
        (pool_hbm, pool_v),
        (table_hbm, table_ref),
        (length_hbm, length_ref),
        (home_hbm, home_ref),
        (choice_hbm, choice_ref),
    )
    loads = [
        pltpu.make_async_copy(source, target, local_sem.at[index])
        for index, (source, target) in enumerate(own)
    ]
    for load in loads:
        load.start()
    loads[0].wait()
    loads[1].wait()
    loads[2].wait()
    loads[7].wait()
    loads[8].wait()
    names[0] = home_ref[...] * 2 + choice_ref[...]
    pl.semaphore_wait(barrier, 7)

    sent = []

    def remote(source, target, send_sem, recv_sem, device):
        copy = pltpu.make_async_remote_copy(
            src_ref=source,
            dst_ref=target,
            send_sem=send_sem,
            recv_sem=recv_sem,
            device_id=device,
            device_id_type=pl.DeviceIdType.MESH,
        )
        copy.start()
        sent.append(copy)
        return copy

    counts = [0, 0]

    def send(source, slot, device):
        at = downs.at[source, slot]
        remote(at, at, piece_send.at[counts[0]], piece_recv.at[source, slot], device)
        counts[0] += 1
        if slot == 0:
            at = ups.at[t, source]
            remote(at, at, up_send.at[counts[1]], up_recv.at[source], device)
            counts[1] += 1

    def landed(target, semaphore):
        pltpu.make_async_copy(target, target, semaphore).wait()

    def arrive(source, slot):
        landed(downs.at[source, slot], piece_recv.at[source, slot])
        if slot == 0:
            landed(ups.at[t, source], up_recv.at[source])

    def pair(source, target, index):
        return remote(source, target, pair_send.at[index], pair_recv.at[index], t_dev)

    near, mid, last = far[1] * 2, far[2] * 2, far[3] * 2
    here = z * 2

    for slot in range(2):
        send(r, slot, x_dev)
    for slot in range(2):
        send(r, slot, z_dev[1])
    remote(names.at[0], names.at[1], cross_send.at[0], cross_recv.at[0], y_dev)
    remote(hidden_v.at[:, theirs], hidden_y, cross_send.at[1], cross_recv.at[1], y_dev)
    for slot in range(2):
        send(r, slot, z_dev[2])
        send(r, slot, z_dev[3])

    loads[3].wait()
    base[0] = jnp.dot(hidden_v[...], weight_v[...], preferred_element_type=jnp.float32)
    base_copy = pair(base.at[0], base.at[1], 0)

    arrive(near + x, 0)
    send(near + x, 0, x_dev)
    arrive(near + x, 1)
    send(near + x, 1, x_dev)
    for load in loads[4:7]:
        load.wait()

    def take_page(entry, carry):
        page = pool_v[table_ref[0, entry]]
        pages_f32[pl.ds(pl.multiple_of(entry * half_block, half_block), half_block), :] = (
            page.astype(jnp.float32)
        )
        return carry

    third = entries // 3
    lax.fori_loop(0, third, take_page, 0, unroll=8)
    arrive(mid + x, 0)
    send(mid + x, 0, x_dev)
    lax.fori_loop(third, 2 * third, take_page, 0, unroll=8)
    arrive(last + x, 0)
    send(last + x, 0, x_dev)
    lax.fori_loop(2 * third, entries, take_page, 0, unroll=8)
    pages[t] = pages_f32[...].astype(jnp.bfloat16)
    pages_copy = pair(pages.at[t], pages.at[t], 1)
    length = fold_columns(length_ref[...], req)
    adapter = fold_columns(names[0], req)
    landed(names.at[1], cross_recv.at[0])
    adapter_y = fold_columns(names[1], req)
    adapters_y = jnp.concatenate([adapter_y] * steps, axis=0)
    lengths = jnp.concatenate([length] * steps, axis=0)
    adapters = jnp.concatenate([adapter] * steps, axis=0)
    step_of = lax.broadcasted_iota(jnp.int32, (rows, 1), 0) // req
    position = (lengths + step_of).astype(jnp.float32)
    lane = lax.broadcasted_iota(jnp.int32, (1, head), 1)
    half = head // 2
    frequency = jnp.exp(
        (lane % half).astype(jnp.float32) * (-2.0 * math.log(rope_base) / head)
    )
    angles = position * frequency
    cosine[...] = jnp.cos(angles)
    sine[...] = jnp.where(lane < half, -jnp.sin(angles), jnp.sin(angles))

    def rotated(vector):
        turned = jnp.concatenate([vector[:, half:], vector[:, :half]], axis=1)
        return vector * cosine[...] + turned * sine[...]

    def rounded(vector):
        return vector.astype(jnp.bfloat16).astype(jnp.float32)

    arrive(mid + x, 1)
    send(mid + x, 1, x_dev)
    base_copy.wait_recv()
    fresh_k[...] = rounded(rotated(base[0, :, head : 2 * head] + base[1, :, head : 2 * head]))
    arrive(last + x, 1)
    send(last + x, 1, x_dev)

    lane_group = lax.broadcasted_iota(jnp.int32, (1, 4 * rank2), 1) // rank2

    def low_part(z_index, lhs, chosen):
        packed = downs[pl.ds(z_index * 2, 2)].reshape(4 * rank2, part_width)
        part = lax.dot_general(
            lhs, packed, (((1,), (1,)), ((), ())), preferred_element_type=jnp.float32
        )
        return jnp.where(chosen == lane_group + 4 * z_index, part, 0.0)

    def spread(part):
        part = part + pltpu.roll(part, 2 * rank2, 1)
        return part + pltpu.roll(part, rank2, 1)

    arrive(here + other_x, 0)
    arrive(here + other_x, 1)
    landed(hidden_y, cross_recv.at[1])
    low_y = low_part(z, hidden_y[...], adapters_y)
    low[0] = low_part(z, hidden_v[:, mine], adapters)
    pages_copy.wait_recv()
    for source in (1, 2):
        arrive(far[source] * 2 + other_x, 0)
        arrive(far[source] * 2 + other_x, 1)
        low_y = low_y + low_part(far[source], hidden_y[...], adapters_y)
        low[0] = low[0] + low_part(far[source], hidden_v[:, mine], adapters)
    arrive(last + other_x, 0)
    up_copy = pair(ups.at[t], ups.at[t], 3)
    arrive(last + other_x, 1)
    low_y = spread(low_y + low_part(far[3], hidden_y[...], adapters_y))
    joined = low_y[:req]
    for s in range(1, steps):
        joined = jnp.where(lane_group == s, low_y[s * req : (s + 1) * req], joined)
    packed_low[0] = joined
    remote(packed_low.at[0], packed_low.at[1], cross_send.at[2], cross_recv.at[2], y_dev)
    remote(packed_low.at[0], packed_low.at[2], cross_send.at[3], cross_recv.at[3], yt_dev)
    low[0] = low[0] + low_part(far[3], hidden_v[:, mine], adapters)
    low_copy = pair(low.at[0], low.at[1], 2)
    up_copy.wait_recv()

    up_full[...] = jnp.zeros_like(up_full)
    for source in range(ups.shape[1]):
        for slot in range(2):
            at = (source * 2 + slot) * rank2
            up_full[at : at + rank, :head] = ups[slot, source, :, :head]
            up_full[at + rank : at + rank2, head:] = ups[slot, source, :, head:]
    low_copy.wait_recv()
    landed(packed_low.at[1], cross_recv.at[2])
    landed(packed_low.at[2], cross_recv.at[3])

    away = packed_low[1] + packed_low[2]
    away = jnp.concatenate(
        [spread(jnp.where(lane_group == s, away, 0.0)) for s in range(steps)], axis=0
    )
    low_sum = low[0] + low[1] + away
    count = up_full.shape[0]
    wide = jnp.concatenate([low_sum] * (count // (4 * rank2)), axis=1)
    owner = lax.broadcasted_iota(jnp.int32, (1, count), 1) // rank2
    wide = jnp.where(adapters == owner, wide, 0.0)
    high = wide.astype(jnp.bfloat16)
    rest = (wide - high.astype(jnp.float32)).astype(jnp.bfloat16)
    term = jnp.dot(high, up_full[...], preferred_element_type=jnp.float32) + jnp.dot(
        rest, up_full[...], preferred_element_type=jnp.float32
    )
    fresh_q[...] = rounded(rotated(base[0, :, :head] + base[1, :, :head] + term[:, :head]))
    fresh_v[...] = base[0, :, 2 * head :] + base[1, :, 2 * head :] + term[:, head:]

    each = 8
    local = steps * each
    span = each * blocks * half_block
    down_row = lax.broadcasted_iota(jnp.int32, (local, 1), 0)
    row_req = down_row % each
    row_step = down_row // each
    column = lax.broadcasted_iota(jnp.int32, (1, 2 * span), 1)
    side = column // span
    inner = column % span
    col_pos = (
        (inner // half_block) % blocks * (2 * half_block) + side * half_block + inner % half_block
    )
    same_old = inner // (blocks * half_block) == row_req
    new_col = lax.broadcasted_iota(jnp.int32, (1, local), 1)
    new_mask = (new_col % each == row_req) & (new_col // each <= row_step)
    scaling = 1.0 / math.sqrt(head)
    contract = (((1,), (1,)), ((), ()))

    for group in range(req // each):
        def picked(ref):
            return jnp.concatenate(
                [ref[s * req + group * each : s * req + (group + 1) * each, :] for s in range(steps)],
                axis=0,
            ).astype(jnp.bfloat16)

        limit = jnp.concatenate([length[group * each : (group + 1) * each]] * steps, axis=0)
        cached = jnp.concatenate(
            [pages[h, group * span : (group + 1) * span, :] for h in range(2)], axis=0
        )
        query, key, value = picked(fresh_q), picked(fresh_k), picked(fresh_v)
        old_mask = same_old & (col_pos < limit)
        old = lax.dot_general(
            query, cached[:, :head], contract, preferred_element_type=jnp.float32
        )
        new = lax.dot_general(query, key, contract, preferred_element_type=jnp.float32)
        old = jnp.where(old_mask, old * scaling, neg_fill)
        new = jnp.where(new_mask, new * scaling, neg_fill)
        peak = jnp.maximum(
            jnp.max(old, axis=1, keepdims=True), jnp.max(new, axis=1, keepdims=True)
        )
        old = jnp.where(old_mask, jnp.exp(old - peak), 0.0)
        new = jnp.where(new_mask, jnp.exp(new - peak), 0.0)
        total = jnp.sum(old, axis=1, keepdims=True) + jnp.sum(new, axis=1, keepdims=True)
        mixed = jnp.dot(
            old.astype(jnp.bfloat16), cached[:, head:], preferred_element_type=jnp.float32
        ) + jnp.dot(new.astype(jnp.bfloat16), value, preferred_element_type=jnp.float32)
        mixed = mixed / total
        for s in range(steps):
            out_ref[s, group * each : (group + 1) * each, :] = mixed[s * each : (s + 1) * each]

    for copy in sent:
        copy.wait_send()


def adapters_to_rows(
    hidden,
    query_key_value_weight,
    adapter_down_weight,
    adapter_up_weight,
    key_value_pool,
    adapter_replica,
    adapter_choice_index,
    cached_length,
    request_block_table,
):
    steps, req, width = hidden.shape
    held, rank, head2 = adapter_up_weight.shape
    head = head2 // 2
    _, entries, half_block, _ = key_value_pool.shape
    replicas = lax.axis_size("replica")
    rows = steps * req
    vmem = pl.BlockSpec(memory_space=pltpu.VMEM)
    hbm = pl.BlockSpec(memory_space=pltpu.HBM)
    sends = 14
    result = pl.pallas_call(
        functools.partial(gather_kernel, steps),
        out_shape=jax.ShapeDtypeStruct((steps, req, head), jnp.float32),
        in_specs=[hbm] * 9,
        out_specs=vmem,
        scratch_shapes=[
            pltpu.VMEM((rows, width), hidden.dtype),
            pltpu.VMEM((width, 3 * head), query_key_value_weight.dtype),
            pltpu.VMEM((entries, half_block, head2), key_value_pool.dtype),
            pltpu.VMEM((1, req), jnp.int32),
            pltpu.VMEM((1, req), jnp.int32),
            pltpu.VMEM((1, req), jnp.int32),
            pltpu.SMEM((1, entries), jnp.int32),
            pltpu.VMEM((entries * half_block, head2), jnp.float32),
            pltpu.VMEM((2, entries * half_block, head2), jnp.bfloat16),
            pltpu.VMEM((replicas, held, 2 * rank, width // 2), jnp.bfloat16),
            pltpu.VMEM((held, replicas, rank, head2), jnp.bfloat16),
            pltpu.VMEM((replicas * held * 2 * rank, head2), jnp.bfloat16),
            pltpu.VMEM((2, rows, 3 * head), jnp.float32),
            pltpu.VMEM((2, rows, 8 * rank), jnp.float32),
            pltpu.VMEM((rows, width // 2), hidden.dtype),
            pltpu.VMEM((2, 1, req), jnp.int32),
            pltpu.VMEM((3, req, 8 * rank), jnp.float32),
            pltpu.VMEM((rows, head), jnp.float32),
            pltpu.VMEM((rows, head), jnp.float32),
            pltpu.VMEM((rows, head), jnp.float32),
            pltpu.VMEM((rows, head), jnp.float32),
            pltpu.VMEM((rows, head), jnp.float32),
            pltpu.SemaphoreType.DMA((9,)),
            pltpu.SemaphoreType.DMA((sends,)),
            pltpu.SemaphoreType.DMA((replicas, held)),
            pltpu.SemaphoreType.DMA((sends // 2,)),
            pltpu.SemaphoreType.DMA((replicas,)),
            pltpu.SemaphoreType.DMA((4,)),
            pltpu.SemaphoreType.DMA((4,)),
            pltpu.SemaphoreType.DMA((4,)),
            pltpu.SemaphoreType.DMA((4,)),
        ],
        compiler_params=pltpu.CompilerParams(
            collective_id=0, has_side_effects=True, vmem_limit_bytes=64 * 1024 * 1024
        ),
    )(
        hidden.reshape(rows, width),
        query_key_value_weight,
        jnp.swapaxes(adapter_down_weight, 1, 2),
        adapter_up_weight,
        key_value_pool[0],
        adapter_replica.reshape(1, req),
        adapter_choice_index.reshape(1, req),
        cached_length,
        request_block_table,
    )
    return result.astype(jnp.bfloat16)


def on_device(*arguments):
    fits = (
        lax.axis_size("replica") == 8
        and lax.axis_size("groups") == 2
        and lax.axis_size("tensor") == 2
        and arguments[3].shape[0] == 2
    )
    return (adapters_to_rows if fits else rows_to_adapters)(*arguments)


def solution(mesh):
    placed = (
        P(None, ("groups", "replica"), "tensor"),
        P("tensor", None),
        P("replica", "tensor", None),
        P("replica", None, None),
        P(("groups", "replica"), None, "tensor", None),
        P(("groups", "replica"), None),
        P(("groups", "replica")),
        P(("groups", "replica"), None),
        P(("groups", "replica"), None),
    )
    return jax.shard_map(
        on_device,
        mesh=mesh,
        in_specs=placed,
        out_specs=P(None, ("groups", "replica"), None),
        check_vma=False,
    )
```

```python
import functools
import math

import jax
import jax.numpy as jnp
from jax import lax
from jax.experimental import pallas as pl
from jax.experimental.pallas import tpu as pltpu
from jax.sharding import PartitionSpec as P

rope_base = 500000.0
neg_fill = -1e30


def combined_all(part, axis, combine):
    gathered = jax.tree.map(lambda a: lax.all_gather(a, axis), part)

    def take(source):
        return jax.tree.map(lambda a: lax.dynamic_index_in_dim(a, source, 0, False), gathered)

    return lax.fori_loop(
        1, lax.axis_size(axis), lambda source, state: combine(state, take(source)), take(0)
    )


def rotate(vector, position):
    half_len = vector.shape[-1] // 2
    frequency = rope_base ** (-(jnp.arange(half_len, dtype=jnp.float32) * 2.0) / vector.shape[-1])
    angles = position[..., None].astype(jnp.float32) * frequency
    cosine = jnp.cos(angles)
    sine_part = jnp.sin(angles)
    first_part = vector[..., :half_len]
    second = vector[..., half_len:]
    return jnp.concatenate(
        [first_part * cosine - second * sine_part, second * cosine + first_part * sine_part],
        axis=-1,
    )


def adapter_delta(row_payload, choice_index, adapter_down_weight, adapter_up_weight):
    req_count, step_count, feat_width = row_payload.shape
    adapter_rank_width = adapter_up_weight.shape[1]
    head_width = adapter_up_weight.shape[2] // 2
    flattened_rows = row_payload.reshape(req_count * step_count, feat_width)
    summed = jnp.zeros((req_count, step_count, 2 * head_width), jnp.float32)
    highest_precision = lax.Precision.HIGHEST
    for adapter_slot in range(adapter_down_weight.shape[0]):
        reduced_rank = jnp.dot(
            flattened_rows, adapter_down_weight[adapter_slot], preferred_element_type=jnp.float32
        ).reshape(req_count, step_count, 2 * adapter_rank_width)
        up_matrix = adapter_up_weight[adapter_slot].astype(jnp.float32)
        query_term = jnp.einsum(
            "nsr,re->nse",
            reduced_rank[..., :adapter_rank_width],
            up_matrix[:, :head_width],
            precision=highest_precision,
        )
        value_term = jnp.einsum(
            "nsr,re->nse",
            reduced_rank[..., adapter_rank_width:],
            up_matrix[:, head_width:],
            precision=highest_precision,
        )
        chosen = (choice_index == adapter_slot)[:, None, None]
        summed = summed + jnp.where(chosen, jnp.concatenate([query_term, value_term], axis=-1), 0.0)
    return summed


def project_input(row_payload, query_key_value_weight, adapter_term):
    req_count, step_count, feat_width = row_payload.shape
    base_part = jnp.dot(
        row_payload.reshape(req_count * step_count, feat_width),
        query_key_value_weight,
        preferred_element_type=jnp.float32,
    ).reshape(req_count, step_count, -1)
    head_width = adapter_term.shape[-1] // 2
    middle_zeros = jnp.zeros(adapter_term.shape[:-1] + (head_width,), jnp.float32)
    return base_part + jnp.concatenate(
        [adapter_term[..., :head_width], middle_zeros, adapter_term[..., head_width:]], axis=-1
    )


def attend(summed, seq_lens, cached, cache_pos, keep_new):
    head_width = cached.shape[-1] // 2
    step_count = summed.shape[1]
    step_ids = jnp.arange(step_count, dtype=jnp.int32)
    position = seq_lens[:, None] + step_ids[None, :]
    queries = rotate(summed[..., :head_width], position).astype(jnp.bfloat16)
    fresh_k = rotate(summed[..., head_width : 2 * head_width], position).astype(jnp.bfloat16)
    fresh_v = summed[..., 2 * head_width :].astype(jnp.bfloat16)
    scaling = 1.0 / math.sqrt(head_width)
    old_scores = (
        jnp.einsum(
            "nsh,nph->nsp", queries, cached[..., :head_width], preferred_element_type=jnp.float32
        )
        * scaling
    )
    new_scores = (
        jnp.einsum("nsh,nth->nst", queries, fresh_k, preferred_element_type=jnp.float32) * scaling
    )
    old_mask = jnp.broadcast_to(
        cache_pos[None, None, :] < seq_lens[:, None, None], old_scores.shape
    )
    new_mask = jnp.broadcast_to(
        (step_ids[None, :, None] >= step_ids[None, None, :]) & keep_new, new_scores.shape
    )
    old_scores = jnp.where(old_mask, old_scores, neg_fill)
    new_scores = jnp.where(new_mask, new_scores, neg_fill)
    peak_val = jnp.maximum(jnp.max(old_scores, axis=-1), jnp.max(new_scores, axis=-1))
    old_exp = jnp.where(old_mask, jnp.exp(old_scores - peak_val[..., None]), 0.0)
    new_exp = jnp.where(new_mask, jnp.exp(new_scores - peak_val[..., None]), 0.0)
    total_sum = jnp.sum(old_exp, axis=-1) + jnp.sum(new_exp, axis=-1)
    accum = jnp.einsum(
        "nsp,nph->nsh",
        old_exp.astype(jnp.bfloat16),
        cached[..., head_width:],
        preferred_element_type=jnp.float32,
    )
    accum = accum + jnp.einsum(
        "nst,nth->nsh", new_exp.astype(jnp.bfloat16), fresh_v, preferred_element_type=jnp.float32
    )
    return (peak_val, total_sum, accum)


def combine(first_part, second):
    peak_val = jnp.maximum(first_part[0], second[0])
    left_scale = jnp.exp(first_part[0] - peak_val)
    right_scale = jnp.exp(second[0] - peak_val)
    return (
        peak_val,
        first_part[1] * left_scale + second[1] * right_scale,
        first_part[2] * left_scale[..., None] + second[2] * right_scale[..., None],
    )


def serve_rows(value_partial, seq_lens, cached, cache_pos, keep_new):
    summed = lax.psum(value_partial, "tensor")
    stats = attend(summed, seq_lens, cached, cache_pos, keep_new)
    peak_val, total_sum, accum = combined_all(stats, "tensor", combine)
    return (accum / total_sum[..., None]).astype(jnp.bfloat16)


def rows_to_adapters(
    hidden,
    query_key_value_weight,
    adapter_down_weight,
    adapter_up_weight,
    key_value_pool,
    adapter_replica,
    adapter_choice_index,
    cached_length,
    request_block_table,
):
    step_count, req_count, feat_width = hidden.shape
    half_len = key_value_pool.shape[2]
    head_width = key_value_pool.shape[3] // 2
    blocks = request_block_table.shape[1] // req_count
    replica_count = lax.axis_size("replica")
    slot_cap = max(2, (2 * req_count + replica_count - 1) // replica_count)
    tensor_id = lax.axis_index("tensor")
    keep_new = tensor_id == 0
    cache_pos = (
        jnp.arange(blocks, dtype=jnp.int32)[:, None] * (half_len * lax.axis_size("tensor"))
        + tensor_id * half_len
        + jnp.arange(half_len, dtype=jnp.int32)[None, :]
    ).reshape(-1)
    seq_lens = cached_length[0]
    home_rep = adapter_replica[:, 0]
    order_idx = jnp.arange(req_count, dtype=jnp.int32)
    earlier = (home_rep[:, None] == home_rep[None, :]) & (order_idx[None, :] < order_idx[:, None])
    slot_of = home_rep * slot_cap + jnp.sum(earlier.astype(jnp.int32), axis=1)
    slot_total = replica_count * slot_cap
    local_rows = jnp.swapaxes(hidden, 0, 1)
    row_buffer = (
        jnp.zeros((slot_total, step_count, feat_width), hidden.dtype).at[slot_of].set(local_rows)
    )
    cached = key_value_pool[0][request_block_table[0].reshape(req_count, blocks)].reshape(
        req_count, blocks * half_len, 2 * head_width
    )
    cache_buffer = (
        jnp.zeros((slot_total, blocks * half_len, 2 * head_width), key_value_pool.dtype)
        .at[slot_of]
        .set(cached)
    )
    meta_ints = (
        jnp.zeros((slot_total, 2), jnp.int32)
        .at[slot_of]
        .set(jnp.stack([adapter_choice_index, seq_lens], axis=1))
    )
    landed_rows, arrived_cache, landed_integers = (
        lax.all_to_all(row_buffer, "replica", split_axis=0, concat_axis=0, tiled=True),
        lax.all_to_all(cache_buffer, "replica", split_axis=0, concat_axis=0, tiled=True),
        lax.all_to_all(meta_ints, "replica", split_axis=0, concat_axis=0, tiled=True),
    )
    adapter_term = adapter_delta(
        landed_rows, landed_integers[:, 0], adapter_down_weight, adapter_up_weight
    )
    value_partial = project_input(landed_rows, query_key_value_weight, adapter_term)
    result = serve_rows(value_partial, landed_integers[:, 1], arrived_cache, cache_pos, keep_new)
    returned = lax.all_to_all(result, "replica", split_axis=0, concat_axis=0, tiled=True)
    return jnp.swapaxes(returned[slot_of], 0, 1)


def fold_columns(row, count):
    down = lax.broadcasted_iota(jnp.int32, (count, count), 0)
    along = lax.broadcasted_iota(jnp.int32, (count, count), 1)
    return jnp.sum(jnp.where(down == along, row, 0), axis=1, keepdims=True)


def gather_kernel(
    steps,
    hidden_hbm,
    weight_hbm,
    down_hbm,
    up_hbm,
    pool_hbm,
    home_hbm,
    choice_hbm,
    length_hbm,
    table_hbm,
    out_ref,
    hidden_v,
    weight_v,
    pool_v,
    home_ref,
    choice_ref,
    length_ref,
    table_ref,
    pages_f32,
    pages,
    downs,
    ups,
    up_full,
    base,
    low,
    hidden_y,
    names,
    packed_low,
    bias,
    new_bias,
    fresh_q,
    fresh_k,
    fresh_v,
    cosine,
    sine,
    local_sem,
    piece_send,
    piece_recv,
    up_send,
    up_recv,
    pair_send,
    pair_recv,
    cross_send,
    cross_recv,
    relay_send,
    relay_up_send,
):
    rows, width = hidden_v.shape
    req = rows // steps
    head = base.shape[2] // 3
    half_block = pool_v.shape[1]
    entries = pool_v.shape[0]
    blocks = entries // req
    rank2 = downs.shape[2]
    rank = rank2 // 2
    g = lax.axis_index("groups")
    r = lax.axis_index("replica")
    t = lax.axis_index("tensor")
    z = r // 2
    x = r % 2
    far = {1: z + 1 - 2 * (z % 2), 2: (z + 2) % 4, 3: 3 - z}
    other_x = 1 - x
    z_dev = {d: {"replica": far[d] * 2 + x} for d in far}
    x_dev = {"replica": z * 2 + other_x}
    y_dev = {"groups": 1 - g}
    t_dev = {"tensor": 1 - t}
    yt_dev = {"groups": 1 - g, "tensor": 1 - t}
    part_width = width // 2
    mine = pl.ds(pl.multiple_of(g * part_width, part_width), part_width)
    theirs = pl.ds(pl.multiple_of((1 - g) * part_width, part_width), part_width)

    barrier = pltpu.get_barrier_semaphore()
    for peer in (z_dev[1], z_dev[2], z_dev[3], x_dev, y_dev, t_dev, yt_dev):
        pl.semaphore_signal(barrier, inc=1, device_id=peer, device_id_type=pl.DeviceIdType.MESH)

    own = (
        (down_hbm.at[:, :, mine], downs.at[r]),
        (up_hbm.at[t], ups.at[t, r]),
        (hidden_hbm, hidden_v),
        (weight_hbm, weight_v),
        (pool_hbm, pool_v),
        (table_hbm, table_ref),
        (length_hbm, length_ref),
        (home_hbm, home_ref),
        (choice_hbm, choice_ref),
    )
    loads = [
        pltpu.make_async_copy(source, target, local_sem.at[index])
        for index, (source, target) in enumerate(own)
    ]
    for load in loads:
        load.start()
    loads[0].wait()
    loads[1].wait()
    loads[2].wait()
    loads[7].wait()
    loads[8].wait()
    names[0] = home_ref[...] * 2 + choice_ref[...]
    pl.semaphore_wait(barrier, 7)

    sent = []

    def remote(source, target, send_sem, recv_sem, device):
        copy = pltpu.make_async_remote_copy(
            src_ref=source,
            dst_ref=target,
            send_sem=send_sem,
            recv_sem=recv_sem,
            device_id=device,
            device_id_type=pl.DeviceIdType.MESH,
        )
        copy.start()
        sent.append(copy)
        return copy

    counts = [0, 0]

    def send(source, slot, device):
        at = downs.at[source, slot]
        remote(at, at, piece_send.at[counts[0]], piece_recv.at[source, slot], device)
        counts[0] += 1
        if slot == 0:
            at = ups.at[t, source]
            remote(at, at, up_send.at[counts[1]], up_recv.at[source], device)
            counts[1] += 1

    def landed(target, semaphore):
        pltpu.make_async_copy(target, target, semaphore).wait()

    def arrive(source, slot):
        landed(downs.at[source, slot], piece_recv.at[source, slot])
        if slot == 0:
            landed(ups.at[t, source], up_recv.at[source])

    def pair(source, target, index):
        return remote(source, target, pair_send.at[index], pair_recv.at[index], t_dev)

    first_z = 2 - z // 2
    second_z = 3 * (1 - z // 2)
    near, mid, last = far[1] * 2, first_z * 2, second_z * 2
    inner = (z + 1) // 2 == 1
    relays = []

    def relay(source, slot, device):
        index = len(relays)
        at = downs.at[source, slot]
        copies = [
            pltpu.make_async_remote_copy(
                src_ref=at,
                dst_ref=at,
                send_sem=relay_send.at[index],
                recv_sem=piece_recv.at[source, slot],
                device_id=device,
                device_id_type=pl.DeviceIdType.MESH,
            )
        ]
        if slot == 0:
            at = ups.at[t, source]
            copies.append(
                pltpu.make_async_remote_copy(
                    src_ref=at,
                    dst_ref=at,
                    send_sem=relay_up_send.at[index],
                    recv_sem=up_recv.at[source],
                    device_id=device,
                    device_id_type=pl.DeviceIdType.MESH,
                )
            )
        relays.append(copies)

        @pl.when(inner)
        def _():
            for copy in copies:
                copy.start()

    here = z * 2

    for slot in range(2):
        send(r, slot, x_dev)
    for slot in range(2):
        send(r, slot, z_dev[1])
    remote(names.at[0], names.at[1], cross_send.at[0], cross_recv.at[0], y_dev)
    for slot in range(2):
        relay(r, slot, z_dev[3])
    remote(hidden_v.at[:, theirs], hidden_y, cross_send.at[1], cross_recv.at[1], y_dev)

    loads[3].wait()
    base[0] = jnp.dot(hidden_v[...], weight_v[...], preferred_element_type=jnp.float32)
    base_copy = pair(base.at[0], base.at[1], 0)

    arrive(near + x, 0)
    relay(near + x, 0, z_dev[3])
    send(near + x, 0, x_dev)
    arrive(near + x, 1)
    relay(near + x, 1, z_dev[3])
    send(near + x, 1, x_dev)
    for load in loads[4:7]:
        load.wait()

    def take_page(entry, carry):
        page = pool_v[table_ref[0, entry]]
        pages_f32[pl.ds(pl.multiple_of(entry * half_block, half_block), half_block), :] = (
            page.astype(jnp.float32)
        )
        return carry

    third = entries // 3
    lax.fori_loop(0, third, take_page, 0, unroll=8)
    arrive(mid + x, 0)
    relay(mid + x, 0, z_dev[1])
    send(mid + x, 0, x_dev)
    lax.fori_loop(third, 2 * third, take_page, 0, unroll=8)
    arrive(mid + x, 1)
    relay(mid + x, 1, z_dev[1])
    send(mid + x, 1, x_dev)
    lax.fori_loop(2 * third, entries, take_page, 0, unroll=8)
    pages[t] = pages_f32[...].astype(jnp.bfloat16)
    pages_copy = pair(pages.at[t], pages.at[t], 1)
    length = fold_columns(length_ref[...], req)
    adapter = fold_columns(names[0], req)
    landed(names.at[1], cross_recv.at[0])
    adapter_y = fold_columns(names[1], req)
    adapters_y = jnp.concatenate([adapter_y] * steps, axis=0)
    lengths = jnp.concatenate([length] * steps, axis=0)
    adapters = jnp.concatenate([adapter] * steps, axis=0)
    step_of = lax.broadcasted_iota(jnp.int32, (rows, 1), 0) // req
    position = (lengths + step_of).astype(jnp.float32)
    lane = lax.broadcasted_iota(jnp.int32, (1, head), 1)
    half = head // 2
    frequency = jnp.exp(
        (lane % half).astype(jnp.float32) * (-2.0 * math.log(rope_base) / head)
    )
    angles = position * frequency
    cosine[...] = jnp.cos(angles)
    sine[...] = jnp.where(lane < half, -jnp.sin(angles), jnp.sin(angles))

    def rotated(vector):
        turned = jnp.concatenate([vector[:, half:], vector[:, :half]], axis=1)
        return vector * cosine[...] + turned * sine[...]

    def rounded(vector):
        return vector.astype(jnp.bfloat16).astype(jnp.float32)

    arrive(last + x, 0)
    relay(last + x, 0, z_dev[1])
    send(last + x, 0, x_dev)
    base_copy.wait_recv()
    fresh_k[...] = rounded(rotated(base[0, :, head : 2 * head] + base[1, :, head : 2 * head]))
    arrive(last + x, 1)
    relay(last + x, 1, z_dev[1])
    send(last + x, 1, x_dev)

    lane_group = lax.broadcasted_iota(jnp.int32, (1, 4 * rank2), 1) // rank2

    def low_part(z_index, lhs, chosen):
        packed = downs[pl.ds(z_index * 2, 2)].reshape(4 * rank2, part_width)
        part = lax.dot_general(
            lhs, packed, (((1,), (1,)), ((), ())), preferred_element_type=jnp.float32
        )
        return jnp.where(chosen == lane_group + 4 * z_index, part, 0.0)

    def spread(part):
        part = part + pltpu.roll(part, 2 * rank2, 1)
        return part + pltpu.roll(part, rank2, 1)

    each = 8
    local = steps * each
    span = each * blocks * half_block
    down_row = lax.broadcasted_iota(jnp.int32, (local, 1), 0)
    row_req = down_row % each
    row_step = down_row // each
    column = lax.broadcasted_iota(jnp.int32, (1, 2 * span), 1)
    side = column // span
    within = column % span
    col_pos = (
        (within // half_block) % blocks * (2 * half_block) + side * half_block + within % half_block
    )
    same_old = within // (blocks * half_block) == row_req
    new_col = lax.broadcasted_iota(jnp.int32, (1, local), 1)
    new_mask = (new_col % each == row_req) & (new_col // each <= row_step)
    scaling = 1.0 / math.sqrt(head)
    contract = (((1,), (1,)), ((), ()))

    for group in range(req // each):
        limit = jnp.concatenate([length[group * each : (group + 1) * each]] * steps, axis=0)
        bias[group] = jnp.where(same_old & (col_pos < limit), 0.0, neg_fill)
    new_bias[...] = jnp.where(new_mask, 0.0, neg_fill)

    arrive(here + other_x, 0)
    arrive(here + other_x, 1)
    landed(hidden_y, cross_recv.at[1])
    low_y = low_part(z, hidden_y[...], adapters_y)
    low[0] = low_part(z, hidden_v[:, mine], adapters)
    pages_copy.wait_recv()
    for source in (far[1], first_z):
        arrive(source * 2 + other_x, 0)
        arrive(source * 2 + other_x, 1)
        low_y = low_y + low_part(source, hidden_y[...], adapters_y)
        low[0] = low[0] + low_part(source, hidden_v[:, mine], adapters)
    arrive(last + other_x, 0)
    up_copy = pair(ups.at[t], ups.at[t], 3)
    arrive(last + other_x, 1)
    low_y = spread(low_y + low_part(second_z, hidden_y[...], adapters_y))
    joined = low_y[:req]
    for s in range(1, steps):
        joined = jnp.where(lane_group == s, low_y[s * req : (s + 1) * req], joined)
    packed_low[0] = joined
    remote(packed_low.at[0], packed_low.at[1], cross_send.at[2], cross_recv.at[2], y_dev)
    remote(packed_low.at[0], packed_low.at[2], cross_send.at[3], cross_recv.at[3], yt_dev)
    low[0] = low[0] + low_part(second_z, hidden_v[:, mine], adapters)
    low_copy = pair(low.at[0], low.at[1], 2)
    up_copy.wait_recv()

    up_full[...] = jnp.zeros_like(up_full)
    for source in range(ups.shape[1]):
        for slot in range(2):
            at = (source * 2 + slot) * rank2
            up_full[at : at + rank, :head] = ups[slot, source, :, :head]
            up_full[at + rank : at + rank2, head:] = ups[slot, source, :, head:]
    low_copy.wait_recv()
    landed(packed_low.at[1], cross_recv.at[2])
    landed(packed_low.at[2], cross_recv.at[3])

    away = packed_low[1] + packed_low[2]
    away = jnp.concatenate(
        [spread(jnp.where(lane_group == s, away, 0.0)) for s in range(steps)], axis=0
    )
    low_sum = low[0] + low[1] + away
    count = up_full.shape[0]
    wide = jnp.concatenate([low_sum] * (count // (4 * rank2)), axis=1)
    owner = lax.broadcasted_iota(jnp.int32, (1, count), 1) // rank2
    wide = jnp.where(adapters == owner, wide, 0.0)
    high = wide.astype(jnp.bfloat16)
    rest = (wide - high.astype(jnp.float32)).astype(jnp.bfloat16)
    term = jnp.dot(high, up_full[...], preferred_element_type=jnp.float32) + jnp.dot(
        rest, up_full[...], preferred_element_type=jnp.float32
    )
    fresh_q[...] = rounded(rotated(base[0, :, :head] + base[1, :, :head] + term[:, :head]))
    fresh_v[...] = base[0, :, 2 * head :] + base[1, :, 2 * head :] + term[:, head:]

    for group in range(req // each):
        def picked(ref):
            return jnp.concatenate(
                [ref[s * req + group * each : s * req + (group + 1) * each, :] for s in range(steps)],
                axis=0,
            ).astype(jnp.bfloat16)

        cached = jnp.concatenate(
            [pages[h, group * span : (group + 1) * span, :] for h in range(2)], axis=0
        )
        query, key, value = picked(fresh_q), picked(fresh_k), picked(fresh_v)
        old = lax.dot_general(
            query, cached[:, :head], contract, preferred_element_type=jnp.float32
        )
        new = lax.dot_general(query, key, contract, preferred_element_type=jnp.float32)
        old = old * scaling + bias[group]
        new = new * scaling + new_bias[...]
        peak = jnp.maximum(
            jnp.max(old, axis=1, keepdims=True), jnp.max(new, axis=1, keepdims=True)
        )
        old = jnp.exp(old - peak)
        new = jnp.exp(new - peak)
        total = jnp.sum(old, axis=1, keepdims=True) + jnp.sum(new, axis=1, keepdims=True)
        mixed = jnp.dot(
            old.astype(jnp.bfloat16), cached[:, head:], preferred_element_type=jnp.float32
        ) + jnp.dot(new.astype(jnp.bfloat16), value, preferred_element_type=jnp.float32)
        mixed = mixed / total
        for s in range(steps):
            out_ref[s, group * each : (group + 1) * each, :] = mixed[s * each : (s + 1) * each]

    for copy in sent:
        copy.wait_send()

    @pl.when(inner)
    def _():
        for copies in relays:
            for copy in copies:
                copy.wait_send()


def adapters_to_rows(
    hidden,
    query_key_value_weight,
    adapter_down_weight,
    adapter_up_weight,
    key_value_pool,
    adapter_replica,
    adapter_choice_index,
    cached_length,
    request_block_table,
):
    steps, req, width = hidden.shape
    held, rank, head2 = adapter_up_weight.shape
    head = head2 // 2
    _, entries, half_block, _ = key_value_pool.shape
    replicas = lax.axis_size("replica")
    rows = steps * req
    vmem = pl.BlockSpec(memory_space=pltpu.VMEM)
    hbm = pl.BlockSpec(memory_space=pltpu.HBM)
    sends = 14
    result = pl.pallas_call(
        functools.partial(gather_kernel, steps),
        out_shape=jax.ShapeDtypeStruct((steps, req, head), jnp.float32),
        in_specs=[hbm] * 9,
        out_specs=vmem,
        scratch_shapes=[
            pltpu.VMEM((rows, width), hidden.dtype),
            pltpu.VMEM((width, 3 * head), query_key_value_weight.dtype),
            pltpu.VMEM((entries, half_block, head2), key_value_pool.dtype),
            pltpu.VMEM((1, req), jnp.int32),
            pltpu.VMEM((1, req), jnp.int32),
            pltpu.VMEM((1, req), jnp.int32),
            pltpu.SMEM((1, entries), jnp.int32),
            pltpu.VMEM((entries * half_block, head2), jnp.float32),
            pltpu.VMEM((2, entries * half_block, head2), jnp.bfloat16),
            pltpu.VMEM((replicas, held, 2 * rank, width // 2), jnp.bfloat16),
            pltpu.VMEM((held, replicas, rank, head2), jnp.bfloat16),
            pltpu.VMEM((replicas * held * 2 * rank, head2), jnp.bfloat16),
            pltpu.VMEM((2, rows, 3 * head), jnp.float32),
            pltpu.VMEM((2, rows, 8 * rank), jnp.float32),
            pltpu.VMEM((rows, width // 2), hidden.dtype),
            pltpu.VMEM((2, 1, req), jnp.int32),
            pltpu.VMEM((3, req, 8 * rank), jnp.float32),
            pltpu.VMEM((req // 8, 8 * steps, entries // req * half_block * 16), jnp.float32),
            pltpu.VMEM((8 * steps, 8 * steps), jnp.float32),
            pltpu.VMEM((rows, head), jnp.float32),
            pltpu.VMEM((rows, head), jnp.float32),
            pltpu.VMEM((rows, head), jnp.float32),
            pltpu.VMEM((rows, head), jnp.float32),
            pltpu.VMEM((rows, head), jnp.float32),
            pltpu.SemaphoreType.DMA((9,)),
            pltpu.SemaphoreType.DMA((sends,)),
            pltpu.SemaphoreType.DMA((replicas, held)),
            pltpu.SemaphoreType.DMA((sends // 2,)),
            pltpu.SemaphoreType.DMA((replicas,)),
            pltpu.SemaphoreType.DMA((4,)),
            pltpu.SemaphoreType.DMA((4,)),
            pltpu.SemaphoreType.DMA((4,)),
            pltpu.SemaphoreType.DMA((4,)),
            pltpu.SemaphoreType.DMA((8,)),
            pltpu.SemaphoreType.DMA((8,)),
        ],
        compiler_params=pltpu.CompilerParams(
            collective_id=0, has_side_effects=True, vmem_limit_bytes=64 * 1024 * 1024
        ),
    )(
        hidden.reshape(rows, width),
        query_key_value_weight,
        jnp.swapaxes(adapter_down_weight, 1, 2),
        adapter_up_weight,
        key_value_pool[0],
        adapter_replica.reshape(1, req),
        adapter_choice_index.reshape(1, req),
        cached_length,
        request_block_table,
    )
    return result.astype(jnp.bfloat16)


def on_device(*arguments):
    fits = (
        lax.axis_size("replica") == 8
        and lax.axis_size("groups") == 2
        and lax.axis_size("tensor") == 2
        and arguments[3].shape[0] == 2
    )
    return (adapters_to_rows if fits else rows_to_adapters)(*arguments)


def solution(mesh):
    placed = (
        P(None, ("groups", "replica"), "tensor"),
        P("tensor", None),
        P("replica", "tensor", None),
        P("replica", None, None),
        P(("groups", "replica"), None, "tensor", None),
        P(("groups", "replica"), None),
        P(("groups", "replica")),
        P(("groups", "replica"), None),
        P(("groups", "replica"), None),
    )
    return jax.shard_map(
        on_device,
        mesh=mesh,
        in_specs=placed,
        out_specs=P(None, ("groups", "replica"), None),
        check_vma=False,
    )
```

```python
import functools
import math

import jax
import jax.numpy as jnp
from jax import lax
from jax.experimental import pallas as pl
from jax.experimental.pallas import tpu as pltpu
from jax.sharding import PartitionSpec as P

rope_base = 500000.0
neg_fill = -1e30


def combined_all(part, axis, combine):
    gathered = jax.tree.map(lambda a: lax.all_gather(a, axis), part)

    def take(source):
        return jax.tree.map(lambda a: lax.dynamic_index_in_dim(a, source, 0, False), gathered)

    return lax.fori_loop(
        1, lax.axis_size(axis), lambda source, state: combine(state, take(source)), take(0)
    )


def rotate(vector, position):
    half_len = vector.shape[-1] // 2
    frequency = rope_base ** (-(jnp.arange(half_len, dtype=jnp.float32) * 2.0) / vector.shape[-1])
    angles = position[..., None].astype(jnp.float32) * frequency
    cosine = jnp.cos(angles)
    sine_part = jnp.sin(angles)
    first_part = vector[..., :half_len]
    second = vector[..., half_len:]
    return jnp.concatenate(
        [first_part * cosine - second * sine_part, second * cosine + first_part * sine_part],
        axis=-1,
    )


def adapter_delta(row_payload, choice_index, adapter_down_weight, adapter_up_weight):
    req_count, step_count, feat_width = row_payload.shape
    adapter_rank_width = adapter_up_weight.shape[1]
    head_width = adapter_up_weight.shape[2] // 2
    flattened_rows = row_payload.reshape(req_count * step_count, feat_width)
    summed = jnp.zeros((req_count, step_count, 2 * head_width), jnp.float32)
    highest_precision = lax.Precision.HIGHEST
    for adapter_slot in range(adapter_down_weight.shape[0]):
        reduced_rank = jnp.dot(
            flattened_rows, adapter_down_weight[adapter_slot], preferred_element_type=jnp.float32
        ).reshape(req_count, step_count, 2 * adapter_rank_width)
        up_matrix = adapter_up_weight[adapter_slot].astype(jnp.float32)
        query_term = jnp.einsum(
            "nsr,re->nse",
            reduced_rank[..., :adapter_rank_width],
            up_matrix[:, :head_width],
            precision=highest_precision,
        )
        value_term = jnp.einsum(
            "nsr,re->nse",
            reduced_rank[..., adapter_rank_width:],
            up_matrix[:, head_width:],
            precision=highest_precision,
        )
        chosen = (choice_index == adapter_slot)[:, None, None]
        summed = summed + jnp.where(chosen, jnp.concatenate([query_term, value_term], axis=-1), 0.0)
    return summed


def project_input(row_payload, query_key_value_weight, adapter_term):
    req_count, step_count, feat_width = row_payload.shape
    base_part = jnp.dot(
        row_payload.reshape(req_count * step_count, feat_width),
        query_key_value_weight,
        preferred_element_type=jnp.float32,
    ).reshape(req_count, step_count, -1)
    head_width = adapter_term.shape[-1] // 2
    middle_zeros = jnp.zeros(adapter_term.shape[:-1] + (head_width,), jnp.float32)
    return base_part + jnp.concatenate(
        [adapter_term[..., :head_width], middle_zeros, adapter_term[..., head_width:]], axis=-1
    )


def attend(summed, seq_lens, cached, cache_pos, keep_new):
    head_width = cached.shape[-1] // 2
    step_count = summed.shape[1]
    step_ids = jnp.arange(step_count, dtype=jnp.int32)
    position = seq_lens[:, None] + step_ids[None, :]
    queries = rotate(summed[..., :head_width], position).astype(jnp.bfloat16)
    fresh_k = rotate(summed[..., head_width : 2 * head_width], position).astype(jnp.bfloat16)
    fresh_v = summed[..., 2 * head_width :].astype(jnp.bfloat16)
    scaling = 1.0 / math.sqrt(head_width)
    old_scores = (
        jnp.einsum(
            "nsh,nph->nsp", queries, cached[..., :head_width], preferred_element_type=jnp.float32
        )
        * scaling
    )
    new_scores = (
        jnp.einsum("nsh,nth->nst", queries, fresh_k, preferred_element_type=jnp.float32) * scaling
    )
    old_mask = jnp.broadcast_to(
        cache_pos[None, None, :] < seq_lens[:, None, None], old_scores.shape
    )
    new_mask = jnp.broadcast_to(
        (step_ids[None, :, None] >= step_ids[None, None, :]) & keep_new, new_scores.shape
    )
    old_scores = jnp.where(old_mask, old_scores, neg_fill)
    new_scores = jnp.where(new_mask, new_scores, neg_fill)
    peak_val = jnp.maximum(jnp.max(old_scores, axis=-1), jnp.max(new_scores, axis=-1))
    old_exp = jnp.where(old_mask, jnp.exp(old_scores - peak_val[..., None]), 0.0)
    new_exp = jnp.where(new_mask, jnp.exp(new_scores - peak_val[..., None]), 0.0)
    total_sum = jnp.sum(old_exp, axis=-1) + jnp.sum(new_exp, axis=-1)
    accum = jnp.einsum(
        "nsp,nph->nsh",
        old_exp.astype(jnp.bfloat16),
        cached[..., head_width:],
        preferred_element_type=jnp.float32,
    )
    accum = accum + jnp.einsum(
        "nst,nth->nsh", new_exp.astype(jnp.bfloat16), fresh_v, preferred_element_type=jnp.float32
    )
    return (peak_val, total_sum, accum)


def combine(first_part, second):
    peak_val = jnp.maximum(first_part[0], second[0])
    left_scale = jnp.exp(first_part[0] - peak_val)
    right_scale = jnp.exp(second[0] - peak_val)
    return (
        peak_val,
        first_part[1] * left_scale + second[1] * right_scale,
        first_part[2] * left_scale[..., None] + second[2] * right_scale[..., None],
    )


def serve_rows(value_partial, seq_lens, cached, cache_pos, keep_new):
    summed = lax.psum(value_partial, "tensor")
    stats = attend(summed, seq_lens, cached, cache_pos, keep_new)
    peak_val, total_sum, accum = combined_all(stats, "tensor", combine)
    return (accum / total_sum[..., None]).astype(jnp.bfloat16)


def rows_to_adapters(
    hidden,
    query_key_value_weight,
    adapter_down_weight,
    adapter_up_weight,
    key_value_pool,
    adapter_replica,
    adapter_choice_index,
    cached_length,
    request_block_table,
):
    step_count, req_count, feat_width = hidden.shape
    half_len = key_value_pool.shape[2]
    head_width = key_value_pool.shape[3] // 2
    blocks = request_block_table.shape[1] // req_count
    replica_count = lax.axis_size("replica")
    slot_cap = max(2, (2 * req_count + replica_count - 1) // replica_count)
    tensor_id = lax.axis_index("tensor")
    keep_new = tensor_id == 0
    cache_pos = (
        jnp.arange(blocks, dtype=jnp.int32)[:, None] * (half_len * lax.axis_size("tensor"))
        + tensor_id * half_len
        + jnp.arange(half_len, dtype=jnp.int32)[None, :]
    ).reshape(-1)
    seq_lens = cached_length[0]
    home_rep = adapter_replica[:, 0]
    order_idx = jnp.arange(req_count, dtype=jnp.int32)
    earlier = (home_rep[:, None] == home_rep[None, :]) & (order_idx[None, :] < order_idx[:, None])
    slot_of = home_rep * slot_cap + jnp.sum(earlier.astype(jnp.int32), axis=1)
    slot_total = replica_count * slot_cap
    local_rows = jnp.swapaxes(hidden, 0, 1)
    row_buffer = (
        jnp.zeros((slot_total, step_count, feat_width), hidden.dtype).at[slot_of].set(local_rows)
    )
    cached = key_value_pool[0][request_block_table[0].reshape(req_count, blocks)].reshape(
        req_count, blocks * half_len, 2 * head_width
    )
    cache_buffer = (
        jnp.zeros((slot_total, blocks * half_len, 2 * head_width), key_value_pool.dtype)
        .at[slot_of]
        .set(cached)
    )
    meta_ints = (
        jnp.zeros((slot_total, 2), jnp.int32)
        .at[slot_of]
        .set(jnp.stack([adapter_choice_index, seq_lens], axis=1))
    )
    landed_rows, arrived_cache, landed_integers = (
        lax.all_to_all(row_buffer, "replica", split_axis=0, concat_axis=0, tiled=True),
        lax.all_to_all(cache_buffer, "replica", split_axis=0, concat_axis=0, tiled=True),
        lax.all_to_all(meta_ints, "replica", split_axis=0, concat_axis=0, tiled=True),
    )
    adapter_term = adapter_delta(
        landed_rows, landed_integers[:, 0], adapter_down_weight, adapter_up_weight
    )
    value_partial = project_input(landed_rows, query_key_value_weight, adapter_term)
    result = serve_rows(value_partial, landed_integers[:, 1], arrived_cache, cache_pos, keep_new)
    returned = lax.all_to_all(result, "replica", split_axis=0, concat_axis=0, tiled=True)
    return jnp.swapaxes(returned[slot_of], 0, 1)


def fold_columns(row, count):
    down = lax.broadcasted_iota(jnp.int32, (count, count), 0)
    along = lax.broadcasted_iota(jnp.int32, (count, count), 1)
    return jnp.sum(jnp.where(down == along, row, 0), axis=1, keepdims=True)


def gather_kernel(
    steps,
    hidden_hbm,
    weight_hbm,
    down_hbm,
    up_hbm,
    pool_hbm,
    home_hbm,
    choice_hbm,
    length_hbm,
    table_hbm,
    out_ref,
    hidden_v,
    weight_v,
    pool_v,
    home_ref,
    choice_ref,
    length_ref,
    table_ref,
    pages_f32,
    pages,
    downs,
    ups,
    up_full,
    base,
    low,
    hidden_y,
    names,
    packed_low,
    bias,
    new_bias,
    fresh_q,
    fresh_k,
    fresh_v,
    cosine,
    sine,
    local_sem,
    piece_send,
    piece_recv,
    up_send,
    up_recv,
    pair_send,
    pair_recv,
    cross_send,
    cross_recv,
    relay_send,
    relay_up_send,
):
    rows, width = hidden_v.shape
    req = rows // steps
    head = base.shape[2] // 3
    half_block = pool_v.shape[1]
    entries = pool_v.shape[0]
    blocks = entries // req
    rank2 = downs.shape[2]
    rank = rank2 // 2
    g = lax.axis_index("groups")
    r = lax.axis_index("replica")
    t = lax.axis_index("tensor")
    z = r // 2
    x = r % 2
    far = {1: z + 1 - 2 * (z % 2), 2: (z + 2) % 4, 3: 3 - z}
    other_x = 1 - x
    z_dev = {d: {"replica": far[d] * 2 + x} for d in far}
    x_dev = {"replica": z * 2 + other_x}
    y_dev = {"groups": 1 - g}
    t_dev = {"tensor": 1 - t}
    yt_dev = {"groups": 1 - g, "tensor": 1 - t}
    part_width = width // 2
    mine = pl.ds(pl.multiple_of(g * part_width, part_width), part_width)
    theirs = pl.ds(pl.multiple_of((1 - g) * part_width, part_width), part_width)

    barrier = pltpu.get_barrier_semaphore()
    for peer in (z_dev[1], z_dev[2], z_dev[3], x_dev, y_dev, t_dev, yt_dev):
        pl.semaphore_signal(barrier, inc=1, device_id=peer, device_id_type=pl.DeviceIdType.MESH)

    own = (
        (down_hbm.at[:, :, mine], downs.at[r]),
        (up_hbm.at[t], ups.at[t, r]),
        (hidden_hbm, hidden_v),
        (weight_hbm, weight_v),
        (pool_hbm, pool_v),
        (table_hbm, table_ref),
        (length_hbm, length_ref),
        (home_hbm, home_ref),
        (choice_hbm, choice_ref),
    )
    loads = [
        pltpu.make_async_copy(source, target, local_sem.at[index])
        for index, (source, target) in enumerate(own)
    ]
    for load in loads:
        load.start()
    loads[0].wait()
    loads[1].wait()
    loads[2].wait()
    loads[7].wait()
    loads[8].wait()
    names[0] = home_ref[...] * 2 + choice_ref[...]
    pl.semaphore_wait(barrier, 7)

    sent = []

    def remote(source, target, send_sem, recv_sem, device):
        copy = pltpu.make_async_remote_copy(
            src_ref=source,
            dst_ref=target,
            send_sem=send_sem,
            recv_sem=recv_sem,
            device_id=device,
            device_id_type=pl.DeviceIdType.MESH,
        )
        copy.start()
        sent.append(copy)
        return copy

    counts = [0, 0]

    def send(source, slot, device):
        at = downs.at[source, slot]
        remote(at, at, piece_send.at[counts[0]], piece_recv.at[source, slot], device)
        counts[0] += 1
        if slot == 0:
            at = ups.at[t, source]
            remote(at, at, up_send.at[counts[1]], up_recv.at[source], device)
            counts[1] += 1

    def landed(target, semaphore):
        pltpu.make_async_copy(target, target, semaphore).wait()

    def arrive(source, slot):
        landed(downs.at[source, slot], piece_recv.at[source, slot])
        if slot == 0:
            landed(ups.at[t, source], up_recv.at[source])

    def pair(source, target, index):
        return remote(source, target, pair_send.at[index], pair_recv.at[index], t_dev)

    first_z = 2 - z // 2
    second_z = 3 * (1 - z // 2)
    near, mid, last = far[1] * 2, first_z * 2, second_z * 2
    inner = (z + 1) // 2 == 1
    relays = []

    def relay(source, slot, device):
        index = len(relays)
        at = downs.at[source, slot]
        copies = [
            pltpu.make_async_remote_copy(
                src_ref=at,
                dst_ref=at,
                send_sem=relay_send.at[index],
                recv_sem=piece_recv.at[source, slot],
                device_id=device,
                device_id_type=pl.DeviceIdType.MESH,
            )
        ]
        if slot == 0:
            at = ups.at[t, source]
            copies.append(
                pltpu.make_async_remote_copy(
                    src_ref=at,
                    dst_ref=at,
                    send_sem=relay_up_send.at[index],
                    recv_sem=up_recv.at[source],
                    device_id=device,
                    device_id_type=pl.DeviceIdType.MESH,
                )
            )
        relays.append(copies)

        @pl.when(inner)
        def _():
            for copy in copies:
                copy.start()

    here = z * 2

    for slot in range(2):
        send(r, slot, x_dev)
    for slot in range(2):
        send(r, slot, z_dev[1])
    remote(names.at[0], names.at[1], cross_send.at[0], cross_recv.at[0], y_dev)
    for slot in range(2):
        relay(r, slot, z_dev[3])
    remote(hidden_v.at[:, theirs], hidden_y, cross_send.at[1], cross_recv.at[1], y_dev)

    loads[3].wait()
    base[0] = jnp.dot(hidden_v[...], weight_v[...], preferred_element_type=jnp.float32)
    base_copy = pair(base.at[0], base.at[1], 0)

    arrive(near + x, 0)
    relay(near + x, 0, z_dev[3])
    send(near + x, 0, x_dev)
    arrive(near + x, 1)
    relay(near + x, 1, z_dev[3])
    send(near + x, 1, x_dev)
    for load in loads[4:7]:
        load.wait()

    def take_page(entry, carry):
        page = pool_v[table_ref[0, entry]]
        pages_f32[pl.ds(pl.multiple_of(entry * half_block, half_block), half_block), :] = (
            page.astype(jnp.float32)
        )
        return carry

    third = entries // 3
    lax.fori_loop(0, third, take_page, 0, unroll=8)
    arrive(mid + x, 0)
    relay(mid + x, 0, z_dev[1])
    send(mid + x, 0, x_dev)
    lax.fori_loop(third, 2 * third, take_page, 0, unroll=8)
    arrive(mid + x, 1)
    relay(mid + x, 1, z_dev[1])
    send(mid + x, 1, x_dev)
    lax.fori_loop(2 * third, entries, take_page, 0, unroll=8)
    pages[t] = pages_f32[...].astype(jnp.bfloat16)
    pages_copy = pair(pages.at[t], pages.at[t], 1)
    length = fold_columns(length_ref[...], req)
    adapter = fold_columns(names[0], req)
    landed(names.at[1], cross_recv.at[0])
    adapter_y = fold_columns(names[1], req)
    adapters_y = jnp.concatenate([adapter_y] * steps, axis=0)
    lengths = jnp.concatenate([length] * steps, axis=0)
    adapters = jnp.concatenate([adapter] * steps, axis=0)
    step_of = lax.broadcasted_iota(jnp.int32, (rows, 1), 0) // req
    position = (lengths + step_of).astype(jnp.float32)
    lane = lax.broadcasted_iota(jnp.int32, (1, head), 1)
    half = head // 2
    frequency = jnp.exp(
        (lane % half).astype(jnp.float32) * (-2.0 * math.log(rope_base) / head)
    )
    angles = position * frequency
    cosine[...] = jnp.cos(angles)
    sine[...] = jnp.where(lane < half, -jnp.sin(angles), jnp.sin(angles))

    def rotated(vector):
        turned = jnp.concatenate([vector[:, half:], vector[:, :half]], axis=1)
        return vector * cosine[...] + turned * sine[...]

    def rounded(vector):
        return vector.astype(jnp.bfloat16).astype(jnp.float32)

    arrive(last + x, 0)
    relay(last + x, 0, z_dev[1])
    send(last + x, 0, x_dev)
    base_copy.wait_recv()
    fresh_k[...] = rounded(rotated(base[0, :, head : 2 * head] + base[1, :, head : 2 * head]))
    arrive(last + x, 1)
    relay(last + x, 1, z_dev[1])
    send(last + x, 1, x_dev)

    lane_group = lax.broadcasted_iota(jnp.int32, (1, 4 * rank2), 1) // rank2

    def low_part(z_index, lhs, chosen):
        packed = downs[pl.ds(z_index * 2, 2)].reshape(4 * rank2, part_width)
        part = lax.dot_general(
            lhs, packed, (((1,), (1,)), ((), ())), preferred_element_type=jnp.float32
        )
        return jnp.where(chosen == lane_group + 4 * z_index, part, 0.0)

    def spread(part):
        part = part + pltpu.roll(part, 2 * rank2, 1)
        return part + pltpu.roll(part, rank2, 1)

    each = 8
    local = steps * each
    span = each * blocks * half_block
    down_row = lax.broadcasted_iota(jnp.int32, (local, 1), 0)
    row_req = down_row % each
    row_step = down_row // each
    column = lax.broadcasted_iota(jnp.int32, (1, 2 * span), 1)
    side = column // span
    within = column % span
    col_pos = (
        (within // half_block) % blocks * (2 * half_block) + side * half_block + within % half_block
    )
    same_old = within // (blocks * half_block) == row_req
    new_col = lax.broadcasted_iota(jnp.int32, (1, local), 1)
    new_mask = (new_col % each == row_req) & (new_col // each <= row_step)
    scaling = 1.0 / math.sqrt(head)
    contract = (((1,), (1,)), ((), ()))

    for group in range(req // each):
        limit = jnp.concatenate([length[group * each : (group + 1) * each]] * steps, axis=0)
        bias[group] = jnp.where(same_old & (col_pos < limit), 0.0, neg_fill)
    new_bias[...] = jnp.where(new_mask, 0.0, neg_fill)

    arrive(here + other_x, 0)
    arrive(here + other_x, 1)
    landed(hidden_y, cross_recv.at[1])
    low_y = low_part(z, hidden_y[...], adapters_y)
    low[0] = low_part(z, hidden_v[:, mine], adapters)
    pages_copy.wait_recv()
    for source in (far[1], first_z):
        arrive(source * 2 + other_x, 0)
        arrive(source * 2 + other_x, 1)
        low_y = low_y + low_part(source, hidden_y[...], adapters_y)
        low[0] = low[0] + low_part(source, hidden_v[:, mine], adapters)
    arrive(last + other_x, 0)
    up_copy = pair(ups.at[t], ups.at[t], 3)
    arrive(last + other_x, 1)
    low_y = spread(low_y + low_part(second_z, hidden_y[...], adapters_y))
    joined = low_y[:req]
    for s in range(1, steps):
        joined = jnp.where(lane_group == s, low_y[s * req : (s + 1) * req], joined)
    packed_low[0] = joined
    remote(packed_low.at[0], packed_low.at[1], cross_send.at[2], cross_recv.at[2], y_dev)
    remote(packed_low.at[0], packed_low.at[2], cross_send.at[3], cross_recv.at[3], yt_dev)
    low[0] = low[0] + low_part(second_z, hidden_v[:, mine], adapters)
    low_copy = pair(low.at[0], low.at[1], 2)
    up_copy.wait_recv()

    up_full[...] = jnp.zeros_like(up_full)
    for source in range(ups.shape[1]):
        for slot in range(2):
            at = (source * 2 + slot) * rank2
            up_full[at : at + rank, :head] = ups[slot, source, :, :head]
            up_full[at + rank : at + rank2, head:] = ups[slot, source, :, head:]
    low_copy.wait_recv()
    landed(packed_low.at[1], cross_recv.at[2])
    landed(packed_low.at[2], cross_recv.at[3])

    away = packed_low[1] + packed_low[2]
    away = jnp.concatenate(
        [spread(jnp.where(lane_group == s, away, 0.0)) for s in range(steps)], axis=0
    )
    low_sum = low[0] + low[1] + away
    count = up_full.shape[0]
    wide = jnp.concatenate([low_sum] * (count // (4 * rank2)), axis=1)
    owner = lax.broadcasted_iota(jnp.int32, (1, count), 1) // rank2
    wide = jnp.where(adapters == owner, wide, 0.0)
    high = wide.astype(jnp.bfloat16)
    rest = (wide - high.astype(jnp.float32)).astype(jnp.bfloat16)
    term = jnp.dot(high, up_full[...], preferred_element_type=jnp.float32) + jnp.dot(
        rest, up_full[...], preferred_element_type=jnp.float32
    )
    fresh_q[...] = rounded(rotated(base[0, :, :head] + base[1, :, :head] + term[:, :head]))
    fresh_v[...] = base[0, :, 2 * head :] + base[1, :, 2 * head :] + term[:, head:]

    def picked(ref, group):
        return jnp.concatenate(
            [ref[s * req + group * each : s * req + (group + 1) * each, :] for s in range(steps)],
            axis=0,
        ).astype(jnp.bfloat16)

    groups = range(req // each)
    spans = [slice(group * span, (group + 1) * span) for group in groups]
    queries = [picked(fresh_q, group) for group in groups]
    olds, news, totals = [], [], []
    for group in groups:
        keys = jnp.concatenate([pages[h, spans[group], :head] for h in range(2)], axis=0)
        old = lax.dot_general(queries[group], keys, contract, preferred_element_type=jnp.float32)
        new = lax.dot_general(
            queries[group],
            picked(fresh_k, group),
            contract,
            preferred_element_type=jnp.float32,
        )
        olds.append(old * scaling + bias[group])
        news.append(new * scaling + new_bias[...])
    peaks = [
        jnp.maximum(jnp.max(old, axis=1, keepdims=True), jnp.max(new, axis=1, keepdims=True))
        for old, new in zip(olds, news)
    ]
    olds = [jnp.exp(old - peak) for old, peak in zip(olds, peaks)]
    news = [jnp.exp(new - peak) for new, peak in zip(news, peaks)]
    totals = [
        jnp.sum(old, axis=1, keepdims=True) + jnp.sum(new, axis=1, keepdims=True)
        for old, new in zip(olds, news)
    ]
    mixes = []
    for group in groups:
        values = jnp.concatenate([pages[h, spans[group], head:] for h in range(2)], axis=0)
        mixes.append(
            jnp.dot(olds[group].astype(jnp.bfloat16), values, preferred_element_type=jnp.float32)
            + jnp.dot(
                news[group].astype(jnp.bfloat16),
                picked(fresh_v, group),
                preferred_element_type=jnp.float32,
            )
        )
    for group in groups:
        mixed = mixes[group] / totals[group]
        for s in range(steps):
            out_ref[s, group * each : (group + 1) * each, :] = mixed[s * each : (s + 1) * each]

    for copy in sent:
        copy.wait_send()

    @pl.when(inner)
    def _():
        for copies in relays:
            for copy in copies:
                copy.wait_send()


def adapters_to_rows(
    hidden,
    query_key_value_weight,
    adapter_down_weight,
    adapter_up_weight,
    key_value_pool,
    adapter_replica,
    adapter_choice_index,
    cached_length,
    request_block_table,
):
    steps, req, width = hidden.shape
    held, rank, head2 = adapter_up_weight.shape
    head = head2 // 2
    _, entries, half_block, _ = key_value_pool.shape
    replicas = lax.axis_size("replica")
    rows = steps * req
    vmem = pl.BlockSpec(memory_space=pltpu.VMEM)
    hbm = pl.BlockSpec(memory_space=pltpu.HBM)
    sends = 14
    result = pl.pallas_call(
        functools.partial(gather_kernel, steps),
        out_shape=jax.ShapeDtypeStruct((steps, req, head), jnp.float32),
        in_specs=[hbm] * 9,
        out_specs=vmem,
        scratch_shapes=[
            pltpu.VMEM((rows, width), hidden.dtype),
            pltpu.VMEM((width, 3 * head), query_key_value_weight.dtype),
            pltpu.VMEM((entries, half_block, head2), key_value_pool.dtype),
            pltpu.VMEM((1, req), jnp.int32),
            pltpu.VMEM((1, req), jnp.int32),
            pltpu.VMEM((1, req), jnp.int32),
            pltpu.SMEM((1, entries), jnp.int32),
            pltpu.VMEM((entries * half_block, head2), jnp.float32),
            pltpu.VMEM((2, entries * half_block, head2), jnp.bfloat16),
            pltpu.VMEM((replicas, held, 2 * rank, width // 2), jnp.bfloat16),
            pltpu.VMEM((held, replicas, rank, head2), jnp.bfloat16),
            pltpu.VMEM((replicas * held * 2 * rank, head2), jnp.bfloat16),
            pltpu.VMEM((2, rows, 3 * head), jnp.float32),
            pltpu.VMEM((2, rows, 8 * rank), jnp.float32),
            pltpu.VMEM((rows, width // 2), hidden.dtype),
            pltpu.VMEM((2, 1, req), jnp.int32),
            pltpu.VMEM((3, req, 8 * rank), jnp.float32),
            pltpu.VMEM((req // 8, 8 * steps, entries // req * half_block * 16), jnp.float32),
            pltpu.VMEM((8 * steps, 8 * steps), jnp.float32),
            pltpu.VMEM((rows, head), jnp.float32),
            pltpu.VMEM((rows, head), jnp.float32),
            pltpu.VMEM((rows, head), jnp.float32),
            pltpu.VMEM((rows, head), jnp.float32),
            pltpu.VMEM((rows, head), jnp.float32),
            pltpu.SemaphoreType.DMA((9,)),
            pltpu.SemaphoreType.DMA((sends,)),
            pltpu.SemaphoreType.DMA((replicas, held)),
            pltpu.SemaphoreType.DMA((sends // 2,)),
            pltpu.SemaphoreType.DMA((replicas,)),
            pltpu.SemaphoreType.DMA((4,)),
            pltpu.SemaphoreType.DMA((4,)),
            pltpu.SemaphoreType.DMA((4,)),
            pltpu.SemaphoreType.DMA((4,)),
            pltpu.SemaphoreType.DMA((8,)),
            pltpu.SemaphoreType.DMA((8,)),
        ],
        compiler_params=pltpu.CompilerParams(
            collective_id=0, has_side_effects=True, vmem_limit_bytes=64 * 1024 * 1024
        ),
    )(
        hidden.reshape(rows, width),
        query_key_value_weight,
        jnp.swapaxes(adapter_down_weight, 1, 2),
        adapter_up_weight,
        key_value_pool[0],
        adapter_replica.reshape(1, req),
        adapter_choice_index.reshape(1, req),
        cached_length,
        request_block_table,
    )
    return result.astype(jnp.bfloat16)


def on_device(*arguments):
    fits = (
        lax.axis_size("replica") == 8
        and lax.axis_size("groups") == 2
        and lax.axis_size("tensor") == 2
        and arguments[3].shape[0] == 2
    )
    return (adapters_to_rows if fits else rows_to_adapters)(*arguments)


def solution(mesh):
    placed = (
        P(None, ("groups", "replica"), "tensor"),
        P("tensor", None),
        P("replica", "tensor", None),
        P("replica", None, None),
        P(("groups", "replica"), None, "tensor", None),
        P(("groups", "replica"), None),
        P(("groups", "replica")),
        P(("groups", "replica"), None),
        P(("groups", "replica"), None),
    )
    return jax.shard_map(
        on_device,
        mesh=mesh,
        in_specs=placed,
        out_specs=P(None, ("groups", "replica"), None),
        check_vma=False,
    )
```
